32 devices in a mesh: dp: 16 (over z, y, x), tensor: 2 (over core).
Axes of the slice: x: 2, y: 2, z: 4, core: 2. Of those that a mesh axis runs over, the one named last changes fastest.
Arguments:
- tokens: bfloat16 [16, 1024, 768], P('dp', 'tensor'), may hold values from -6 to 6
- temb: bfloat16 [16, 768], P('dp'), may hold values from -6 to 6
- lengths: int32 [16], P('dp'), may hold values from 128 to 1024, as said below
- w_mod: bfloat16 [768, 4608], P('dp'), may hold values from -0.109375 to 0.109375
- b_mod: bfloat16 [4608], replicated, may hold values from -1.796875 to 1.796875
- gain_attn: bfloat16 [768], replicated, may hold values from 0.25 to 1.75
- query_key_value_weight: bfloat16 [768, 3, 768], P(None, None, 'tensor'), may hold values from -0.21875 to 0.21875
- b_qkv: bfloat16 [3, 768], P(None, 'tensor'), may hold values from -1.796875 to 1.796875
- attention_output_weight: bfloat16 [768, 768], P('tensor'), may hold values from -1.25 to 1.25
- gain_mlp: bfloat16 [768], replicated, may hold values from 0.25 to 1.75
- up_weight: bfloat16 [768, 3072], P(None, 'tensor'), may hold values from -0.21875 to 0.21875
- b_up: bfloat16 [3072], P('tensor'), may hold values from -3 to 3
- down_weight: bfloat16 [3072, 768], P('tensor'), may hold values from -0.21875 to 0.21875
- b_down: bfloat16 [768], replicated, may hold values from -1.796875 to 1.796875
- cotangent: bfloat16 [16, 1024, 768], P('dp', 'tensor'), may hold values from -6 to 6
Outputs:
- output: bfloat16 [16, 1024, 768], P('dp', 'tensor')
- grad_tokens: bfloat16 [16, 1024, 768], P('dp', 'tensor')
- grad_temb: float32 [16, 768], P('dp')
- grad_w_mod: float32 [768, 4608], P('dp')
- grad_b_mod: float32 [4608], replicated
- grad_gain_attn: float32 [768], replicated
- grad_w_qkv: float32 [768, 3, 768], P(None, None, 'tensor')
- grad_b_qkv: float32 [3, 768], P(None, 'tensor')
- grad_w_out: float32 [768, 768], P('tensor')
- grad_gain_mlp: float32 [768], replicated
- up_weight_gradient: float32 [768, 3072], P(None, 'tensor')
- grad_b_up: float32 [3072], P('tensor')
- grad_w_down: float32 [3072, 768], P('tensor')
- grad_b_down: float32 [768], replicated
The draws below stay inside these ranges and needn't reach their ends.
Inputs may be any that keep to these rules, and one draw needn't show every extreme that they name: `lengths`: each sequence's count of valid tokens, more of them near the low end; one sequence in all has exactly 1024.
All inputs are finite; a program needn't handle non-finite values.
Results may differ from the reference program's by a relative error of at most 0.018.
Values may be sent and summed in bfloat16 or wider, within the bound.
No kernel may reach another device: no remote copies, remote signals or barrier semaphores. Data moves between devices by JAX's collectives and lax.ppermute only.
A program may use at most 192 MiB of HBM per device.

```python
import math
from functools import partial
import jax
import jax.numpy as jnp
from jax import lax

D = 768
HEADS = 12
HEAD_DIM = 64
FF = 3072
TD = 768
LEN = 1024
LMIN = 128
SEQS = 16


def draw_lengths(key, part):
    key = jax.random.fold_in(key, 7)
    sub_keys = jax.random.split(key, 4)
    span_size = LEN - LMIN + 1
    first_draw = jax.random.randint(sub_keys[0], (SEQS,), 0, span_size)
    second_draw = jax.random.randint(sub_keys[1], (SEQS,), 0, span_size)
    third_draw = jax.random.randint(sub_keys[2], (SEQS,), 0, span_size)
    short_len = LMIN + jnp.minimum(jnp.minimum(first_draw, second_draw), third_draw)
    forced = jax.random.randint(sub_keys[3], (), 0, SEQS)
    return jnp.where(jnp.arange(SEQS) == forced, LEN, short_len).astype(jnp.int32)


def with_spikes(array, stream_key, source, target, blocks, factor):
    def block_of(axis_at):
        return (jnp.arange(array.shape[axis_at]) // (array.shape[axis_at] // blocks)).reshape((-1,) + (1,) * (array.ndim - 1 - axis_at))

    one_side = jax.random.permutation(stream_key, blocks)[block_of(target)]
    second = (block_of(target) + blocks // 2) % blocks
    return jnp.where((block_of(source) == one_side) | (block_of(source) == second), factor * array, array)


def levels(own_key, shape, shards, least, high):
    def one(axis_at, shards_of):
        steps = jax.random.uniform(jax.random.fold_in(jax.random.fold_in(own_key, 6), axis_at), (shards_of,), jnp.float32, least / len(shards), high / len(shards))
        return jnp.repeat(jnp.exp(steps), shape[axis_at] // shards_of).reshape((-1,) + (1,) * (len(shape) - axis_at - 1))

    loudness = one(*shards[0])
    for cut in shards[1:]:
        loudness = loudness * one(*cut)
    return loudness


def normal_values(own_key, shape, deviation, reach, cuts=(), kind=jnp.bfloat16):
    values = jax.random.normal(own_key, shape, jnp.float32) * deviation
    if len(cuts) > 0:
        values = levels(own_key, shape, cuts, -0.22, 0.18) * values
    return jnp.clip(values, min=-reach, max=reach).astype(kind)


def gaussian_with(rng, shape, width, most, cuts, heavy, held_as=jnp.bfloat16):
    entries = width * jax.random.normal(rng, shape, jnp.float32)
    if cuts:
        entries = entries * levels(rng, shape, cuts, -0.22, 0.18)
    return jnp.clip(with_spikes(entries, jax.random.fold_in(rng, 3), *heavy), -most, most).astype(held_as)


def setup_inputs(seed: int = 0) -> dict:
    key_list = jax.random.split(jax.random.key(seed), 16)
    return {
        "tokens": normal_values(key_list[0], (SEQS, LEN, D), 1.0, 6.0, ((0, 16), (1, 2))),
        "temb": gaussian_with(key_list[1], (SEQS, TD), 1.0, 6.0, ((0, 16),), (0, 1, 16, 2.0)),
        "lengths": draw_lengths(jax.random.fold_in(key_list[15], 71), 0),
        "w_mod": normal_values(key_list[3], (TD, 6 * D), (4 * TD) ** -0.5, 0.109375, ((0, 16),)),
        "b_mod": normal_values(key_list[4], (6 * D,), 0.3, 1.796875),
        "gain_attn": jnp.clip(1.0 + 0.15 * jax.random.normal(key_list[5], (D,), jnp.float32), 0.25, 1.75).astype(jnp.bfloat16),
        "query_key_value_weight": normal_values(key_list[6], (D, 3, D), D ** -0.5, 0.21875, ((2, 2),)),
        "b_qkv": normal_values(key_list[7], (3, D), 0.3, 1.796875, ((1, 2),)),
        "attention_output_weight": normal_values(key_list[8], (D, D), (D // 32) ** -0.5, 1.25, ((0, 2),)),
        "gain_mlp": jnp.clip(1.0 + 0.15 * jax.random.normal(key_list[9], (D,), jnp.float32), 0.25, 1.75).astype(jnp.bfloat16),
        "up_weight": normal_values(key_list[10], (D, FF), D ** -0.5, 0.21875, ((1, 2),)),
        "b_up": normal_values(key_list[11], (FF,), 0.5, 3.0, ((0, 2),)),
        "down_weight": normal_values(key_list[12], (FF, D), (FF // 4) ** -0.5, 0.21875, ((0, 2),)),
        "b_down": normal_values(key_list[13], (D,), 0.3, 1.796875),
        "cotangent": normal_values(key_list[14], (SEQS, LEN, D), 1.0, 6.0, ((0, 16), (1, 2))),
    }


@jax.custom_vjp
def low(v):
    return lax.optimization_barrier(v.astype(jnp.bfloat16)).astype(jnp.float32)

@jax.custom_vjp
def low_back(v):
    return v

def low_keep(v):
    return (low(v), None)

def low_pass(kept, grad):
    return (grad,)

def back_keep(v):
    return (v, None)

def back_low(kept, grad):
    return (low(grad),)
low.defvjp(low_keep, low_pass)
low_back.defvjp(back_keep, back_low)

def layer_norm(field):
    centred = field - lax.optimization_barrier(jnp.mean(field, axis=-1, keepdims=True))
    return centred * lax.rsqrt(lax.optimization_barrier(jnp.mean(centred * centred, axis=-1, keepdims=True)) + 1e-05)

def rotary_tables():
    half_size = HEAD_DIM // 2
    frequency = 10000.0 ** (-jnp.arange(half_size, dtype=jnp.float32) / half_size)
    angles = jnp.arange(LEN, dtype=jnp.float32)[:, None] * frequency[None, :]
    return (jnp.cos(angles), jnp.sin(angles))

def rotate(field, cosine, sine):
    half_size = HEAD_DIM // 2
    first_half = field[..., :half_size]
    second_half = field[..., half_size:]
    cosine = cosine[:, None, :]
    sine = sine[:, None, :]
    return jnp.concatenate([first_half * cosine - second_half * sine, second_half * cosine + first_half * sine], axis=-1)

def head_attention(parts, key_valid):
    query, keys, values = parts
    scores = low_back(jnp.einsum('gqe,gke->gqk', query, keys, precision=lax.Precision.HIGHEST) * HEAD_DIM ** (-0.5))
    scores = jnp.where(key_valid[:, None, :], scores, -1e+30)
    row_max = lax.optimization_barrier(jnp.max(scores, axis=-1, keepdims=True))
    weights = jnp.exp(scores - row_max)
    chances = low(weights / lax.optimization_barrier(jnp.sum(weights, axis=-1, keepdims=True)))
    return jnp.einsum('gqk,gke->gqe', chances, values, precision=lax.Precision.HIGHEST)

def forward(key_valid, tokens, temb, w_mod, b_mod, gain_attn, query_key_value_weight, b_qkv, attention_output_weight, gain_mlp, up_weight, b_up, down_weight, b_down):
    modulation = jnp.dot(temb, w_mod, precision=lax.Precision.HIGHEST) + b_mod
    pieces = [modulation[:, None, k * D:(k + 1) * D] for k in range(6)]
    shift_attn, scale_attn, gate_attn, shift_mlp, scale_mlp, gate_mlp = pieces
    group = tokens.shape[0]
    attn_in = low(layer_norm(tokens) * gain_attn * (1.0 + scale_attn) + shift_attn)
    projected = low_back(jnp.einsum('gld,dce->glce', attn_in, query_key_value_weight, precision=lax.Precision.HIGHEST) + b_qkv)
    split_heads = projected.reshape(group, LEN, 3, HEADS, HEAD_DIM)
    cosine, sine = rotary_tables()
    query = low(rotate(split_heads[:, :, 0], cosine, sine))
    keys = low(rotate(split_heads[:, :, 1], cosine, sine))
    values = low(split_heads[:, :, 2])
    attend = jax.checkpoint(partial(head_attention, key_valid=key_valid))
    per_head = lax.map(attend, (jnp.moveaxis(query, 2, 0), jnp.moveaxis(keys, 2, 0), jnp.moveaxis(values, 2, 0)))
    attended = low(low_back(jnp.moveaxis(per_head, 0, 2).reshape(group, LEN, D)))
    attn_branch = low_back(jnp.einsum('gle,ed->gld', attended, attention_output_weight, precision=lax.Precision.HIGHEST))
    middle = tokens + gate_attn * attn_branch
    mlp_in = low(layer_norm(middle) * gain_mlp * (1.0 + scale_mlp) + shift_mlp)
    hidden = low_back(jnp.einsum('gld,df->glf', mlp_in, up_weight, precision=lax.Precision.HIGHEST) + b_up)
    active_rows_mask = low(jax.nn.gelu(hidden, approximate=True))
    mlp_branch = low_back(jnp.einsum('glf,fd->gld', active_rows_mask, down_weight, precision=lax.Precision.HIGHEST) + b_down)
    row_valid = key_valid[..., None].astype(jnp.float32)
    return (middle + gate_mlp * mlp_branch) * row_valid

def reference(tokens, temb, lengths, w_mod, b_mod, gain_attn, query_key_value_weight, b_qkv, attention_output_weight, gain_mlp, up_weight, b_up, down_weight, b_down, cotangent):
    group = math.gcd(SEQS, max(1, 4096 // LEN))
    turns = SEQS // group
    params = tuple((p.astype(jnp.float32) for p in (w_mod, b_mod, gain_attn, query_key_value_weight, b_qkv, attention_output_weight, gain_mlp, up_weight, b_up, down_weight, b_down)))
    positions = jnp.arange(LEN, dtype=jnp.int32)

    def one_group(running, pieces):
        token_part, embed_part, length_part, cot_part = pieces
        key_valid = positions[None, :] < length_part[:, None]
        result, pullback = jax.vjp(partial(forward, key_valid), token_part.astype(jnp.float32), embed_part.astype(jnp.float32), *params)
        gradients = pullback(cot_part.astype(jnp.float32))
        running = tuple((carried + gradient for carried, gradient in zip(running, gradients[2:])))
        return (running, (result.astype(jnp.bfloat16), gradients[0].astype(jnp.bfloat16), gradients[1]))
    zero_totals = tuple((jnp.zeros_like(p) for p in params))
    stacked = (tokens.reshape(turns, group, LEN, D), temb.reshape(turns, group, TD), lengths.reshape(turns, group), cotangent.reshape(turns, group, LEN, D))
    totals, (outputs, token_grads, embed_grads) = lax.scan(one_group, zero_totals, stacked)
    return (outputs.reshape(SEQS, LEN, D), token_grads.reshape(SEQS, LEN, D), embed_grads.reshape(SEQS, TD), totals[0], totals[1], totals[2], totals[3], totals[4], totals[5], totals[6], totals[7], totals[8], totals[9], totals[10])
```

```python
from math import sqrt, pi

import jax
import jax.numpy as jnp
from jax import lax
from jax.sharding import PartitionSpec as P

HEAD_DIM = 64
F32 = jnp.float32
BF16 = jnp.bfloat16


def norm_parts(field):
    centred = field - jnp.mean(field, axis=-1, keepdims=True)
    inverse = lax.rsqrt(jnp.mean(centred * centred, axis=-1, keepdims=True) + 1e-05)
    return (centred * inverse, inverse)


def norm_back(upstream, normed, inverse):
    return inverse * (
        upstream
        - jnp.mean(upstream, axis=-1, keepdims=True)
        - normed * jnp.mean(upstream * normed, axis=-1, keepdims=True)
    )


def rotary_tables(start, rows):
    half_size = HEAD_DIM // 2
    frequency = 10000.0 ** (-lax.iota(F32, half_size) / half_size)
    places = (start + lax.iota(jnp.int32, rows)).astype(F32)
    angles = places[:, None] * frequency[None, :]
    return (jnp.cos(angles), jnp.sin(angles))


def rotate(field, cosine, sine, direction):
    half_size = field.shape[-1] // 2
    first_half = field[..., :half_size]
    second_half = field[..., half_size:]
    cosine = cosine[:, None, :]
    sine = direction * sine[:, None, :]
    return jnp.concatenate(
        [first_half * cosine - second_half * sine, second_half * cosine + first_half * sine],
        axis=-1,
    )


def gelu_parts(hidden):
    scale = sqrt(2.0 / pi)
    square = hidden * hidden
    bent = jnp.tanh(scale * hidden * (1.0 + 0.044715 * square))
    upper = 0.5 * (1.0 + bent)
    slope = upper + 0.5 * hidden * (1.0 - bent * bent) * scale * (1.0 + 3 * 0.044715 * square)
    return (hidden * upper, slope)


def dot(left, right, dims):
    return lax.dot_general(left, right, (dims, ((), ())), preferred_element_type=F32)


def swap(value):
    return lax.ppermute(value, "tensor", [(0, 1), (1, 0)])


def bit_swap(value, bit, order_by_core):
    pairs = []
    for place in range(lax.axis_size("dp")):
        for core in range(2):
            use = bit ^ core if order_by_core else bit
            pairs.append((place * 2 + core, (place ^ (1 << use)) * 2 + core))
    return lax.ppermute(value, ("dp", "tensor"), pairs)


def pick(value, index):
    return lax.dynamic_index_in_dim(value, index, 0, keepdims=False)


def join(mine, other, index):
    return jnp.where(index == 0, jnp.stack([mine, other]), jnp.stack([other, mine]))


def add_low(mine, other):
    return (mine.astype(F32) + other.astype(F32)).astype(BF16)


def bit_count():
    return lax.axis_size("dp").bit_length() - 1


def reduce_over_dp(parts):
    place = lax.axis_index("dp")
    core = lax.axis_index("tensor")
    first = (place >> core) & 1
    second = (place >> (1 - core)) & 1
    shape = parts.shape
    parts = parts.reshape((2, 2, shape[0] // 4) + shape[1:])
    half = add_low(pick(parts, first), bit_swap(pick(parts, 1 - first), 0, True))
    quarter = add_low(pick(half, second), bit_swap(pick(half, 1 - second), 1, True))
    for bit in range(2, bit_count()):
        quarter = add_low(quarter, bit_swap(quarter, bit, False))
    half = join(quarter, bit_swap(quarter, 1, True), second)
    parts = join(half, bit_swap(half, 0, True), first)
    return parts.reshape(shape)


def gather_over_dp(value):
    place = lax.axis_index("dp")
    value = value[None]
    for bit in range(bit_count()):
        other = bit_swap(value, bit, False)
        value = join(value, other, (place >> bit) & 1).reshape((-1,) + value.shape[1:])
    return value


def shards(
    tokens,
    temb,
    lengths,
    w_mod,
    b_mod,
    gain_attn,
    query_key_value_weight,
    b_qkv,
    attention_output_weight,
    gain_mlp,
    up_weight,
    b_up,
    down_weight,
    b_down,
    cotangent,
):
    tokens, cotangent, length = tokens[0], cotangent[0], lengths[0]
    rows, width = tokens.shape
    core = lax.axis_index("tensor")
    half_width = width // 2
    heads = half_width // HEAD_DIM
    score_scale = HEAD_DIM ** (-0.5)
    start = core * rows
    row_valid = ((start + lax.iota(jnp.int32, rows)) < length).astype(F32)[:, None]
    far_valid = ((rows - start) + lax.iota(jnp.int32, rows)) < length
    key_valid = jnp.concatenate([row_valid[:, 0] > 0, far_valid])

    qkv_own = jnp.swapaxes(query_key_value_weight, 0, 1)
    qkv_w = [qkv_own, swap(qkv_own)]
    out_w = [attention_output_weight, swap(attention_output_weight)]
    up_w = [up_weight, swap(up_weight)]
    down_w = [down_weight, swap(down_weight)]
    biases = jnp.concatenate([b_qkv.reshape(-1), b_up])
    biases_far = swap(biases)
    qkv_size = 3 * half_width
    qkv_b = [b.reshape(3, half_width).astype(F32) for b in (biases[:qkv_size], biases_far[:qkv_size])]
    up_b = [b.astype(F32) for b in (biases[qkv_size:], biases_far[qkv_size:])]

    embed_part = lax.all_to_all(temb, "dp", split_axis=1, concat_axis=0, tiled=True)
    mod_terms = jnp.dot(embed_part, w_mod, preferred_element_type=F32)
    mod_terms = lax.all_to_all(mod_terms, "dp", split_axis=0, concat_axis=0, tiled=True)
    modulation = jnp.sum(mod_terms, axis=0) + b_mod.astype(F32)
    shift_attn, scale_attn, gate_attn, shift_mlp, scale_mlp, gate_mlp = [
        modulation[None, k * width : (k + 1) * width] for k in range(6)
    ]
    gain_attn = gain_attn.astype(F32)[None]
    gain_mlp = gain_mlp.astype(F32)[None]
    factor_attn = gain_attn * (1.0 + scale_attn)
    factor_mlp = gain_mlp * (1.0 + scale_mlp)

    inputs = tokens.astype(F32)
    normed_attn, inverse_attn = norm_parts(inputs)
    attn_in = (normed_attn * factor_attn + shift_attn).astype(BF16)
    cosine, sine = rotary_tables(start, rows)
    queries, keys, values = [], [], []
    for weight, bias in zip(qkv_w, qkv_b):
        query, key, value = [
            (dot(attn_in, weight[c], ((1,), (0,))) + bias[c][None]).reshape(rows, heads, HEAD_DIM)
            for c in range(3)
        ]
        queries.append(rotate(query, cosine, sine, 1.0).astype(BF16))
        keys.append(rotate(key, cosine, sine, 1.0).astype(BF16))
        values.append(value.astype(BF16))
    query = jnp.concatenate(queries, axis=1)
    near = jnp.stack([jnp.stack([keys[p], values[p]]) for p in range(2)])
    far = swap(near)
    key = jnp.concatenate(
        [jnp.concatenate([near[0, 0], near[1, 0]], 1), jnp.concatenate([far[1, 0], far[0, 0]], 1)], 0
    )
    value = jnp.concatenate(
        [jnp.concatenate([near[0, 1], near[1, 1]], 1), jnp.concatenate([far[1, 1], far[0, 1]], 1)], 0
    )

    scores = jnp.einsum("qhe,khe->hqk", query, key, preferred_element_type=F32) * score_scale
    scores = jnp.where(key_valid[None, None, :], scores, -1e30)
    weights = jnp.exp(scores - jnp.max(scores, axis=-1, keepdims=True))
    probability = weights / jnp.sum(weights, axis=-1, keepdims=True)
    chances = probability.astype(BF16)
    attended = jnp.einsum("hqk,khe->qhe", chances, value, preferred_element_type=F32).astype(BF16)
    attended_flat = [
        attended[:, p * heads : (p + 1) * heads].reshape(rows, half_width) for p in range(2)
    ]
    attn_branch = sum(dot(a, w, ((1,), (0,))) for a, w in zip(attended_flat, out_w))
    middle = inputs + gate_attn * attn_branch
    normed_mlp, inverse_mlp = norm_parts(middle)
    mlp_in = (normed_mlp * factor_mlp + shift_mlp).astype(BF16)

    d_result = cotangent.astype(F32) * row_valid
    g_mlp = (d_result * gate_mlp).astype(BF16)
    actives, slopes, grad_down = [], [], []
    for weight, bias in zip(up_w, up_b):
        active, slope = gelu_parts(dot(mlp_in, weight, ((1,), (0,))) + bias[None])
        actives.append(active.astype(BF16))
        slopes.append(slope)
    grad_down = [dot(a, g_mlp, ((0,), (0,))).astype(BF16) for a in actives]
    down_sum = add_low(grad_down[0], swap(grad_down[1]))
    down_total = reduce_over_dp(down_sum)
    d_hidden = [
        (dot(g_mlp, w, ((1,), (1,))) * s).astype(BF16) for w, s in zip(down_w, slopes)
    ]
    grad_up = [dot(mlp_in, d, ((0,), (0,))).astype(BF16) for d in d_hidden]
    up_sum = add_low(grad_up[0], swap(grad_up[1]))
    up_total = reduce_over_dp(up_sum)
    grad_b_up = [jnp.sum(d, axis=0, dtype=F32) for d in d_hidden]
    d_mlp_in = sum(dot(d, w, ((1,), (1,))) for d, w in zip(d_hidden, up_w))
    mlp_branch = sum(dot(a, w, ((1,), (0,))) for a, w in zip(actives, down_w))
    mlp_branch = mlp_branch + b_down.astype(F32)[None]
    output = ((middle + gate_mlp * mlp_branch) * row_valid).astype(BF16)
    grad_gate_mlp = jnp.sum(d_result * mlp_branch, axis=0)
    grad_b_down = jnp.sum(g_mlp, axis=0, dtype=F32)
    d_middle = d_result + norm_back(d_mlp_in * factor_mlp, normed_mlp, inverse_mlp)
    grad_shift_mlp = jnp.sum(d_mlp_in, axis=0)
    d_norm = jnp.sum(d_mlp_in * normed_mlp, axis=0)
    grad_scale_mlp = d_norm * gain_mlp[0]
    grad_gain_mlp = d_norm * (1.0 + scale_mlp[0])
    grad_gate_attn = jnp.sum(d_middle * attn_branch, axis=0)
    g_attn = (d_middle * gate_attn).astype(BF16)
    grad_out = [dot(a, g_attn, ((0,), (0,))).astype(BF16) for a in attended_flat]
    d_attended = jnp.concatenate(
        [dot(g_attn, w, ((1,), (1,))).astype(BF16).reshape(rows, heads, HEAD_DIM) for w in out_w], 1
    )

    d_chances = jnp.einsum("qhe,khe->hqk", d_attended, value, preferred_element_type=F32)
    d_scores = (
        probability * (d_chances - jnp.sum(probability * d_chances, axis=-1, keepdims=True))
    ).astype(BF16)
    d_query = jnp.einsum("hqk,khe->qhe", d_scores, key, preferred_element_type=F32) * score_scale
    d_key = jnp.einsum("hqk,qhe->khe", d_scores, query, preferred_element_type=F32) * score_scale
    d_value = jnp.einsum("hqk,qhe->khe", chances, d_attended, preferred_element_type=F32)
    d_far = jnp.stack([d_key[rows:], d_value[rows:]]).astype(BF16)
    d_far = jnp.stack([d_far[:, :, heads:], d_far[:, :, :heads]])
    d_back = swap(d_far).astype(F32)
    grad_qkv, grad_b_qkv = [], []
    d_attn_in = 0.0
    for p in range(2):
        of = slice(p * heads, (p + 1) * heads)
        parts = [
            rotate(d_query[:, of], cosine, sine, -1.0),
            rotate(d_key[:rows, of] + d_back[p, 0], cosine, sine, -1.0),
            d_value[:rows, of] + d_back[p, 1],
        ]
        parts = [d.reshape(rows, half_width).astype(BF16) for d in parts]
        grad_qkv.append(jnp.stack([dot(attn_in, d, ((0,), (0,))).astype(BF16) for d in parts]))
        grad_b_qkv.append(jnp.concatenate([jnp.sum(d, axis=0, dtype=F32) for d in parts]))
        d_attn_in = d_attn_in + sum(
            dot(d, qkv_w[p][c], ((1,), (1,))) for c, d in enumerate(parts)
        )
    mixed = [
        jnp.concatenate([q.reshape(3 * width, half_width), o.reshape(width, half_width)])
        for q, o in zip(grad_qkv, grad_out)
    ]
    mixed_total = reduce_over_dp(add_low(mixed[0], swap(mixed[1]))).astype(F32)
    qkv_total = jnp.swapaxes(mixed_total[: 3 * width].reshape(3, width, half_width), 0, 1)
    out_total = mixed_total[3 * width :].reshape(half_width, width)

    grad_shift_attn = jnp.sum(d_attn_in, axis=0)
    d_norm = jnp.sum(d_attn_in * normed_attn, axis=0)
    grad_scale_attn = d_norm * gain_attn[0]
    grad_gain_attn = d_norm * (1.0 + scale_attn[0])
    grad_tokens = (d_middle + norm_back(d_attn_in * factor_attn, normed_attn, inverse_attn)).astype(BF16)

    shared = jnp.concatenate(
        [
            grad_shift_attn,
            grad_scale_attn,
            grad_gate_attn,
            grad_shift_mlp,
            grad_scale_mlp,
            grad_gate_mlp,
            grad_gain_attn,
            grad_gain_mlp,
            grad_b_down,
            jnp.zeros_like(grad_b_down),
        ]
    ).reshape(2, -1)
    mine = jnp.concatenate([pick(shared, core), grad_b_qkv[0], grad_b_up[0]])
    yours = jnp.concatenate([pick(shared, 1 - core), grad_b_qkv[1], grad_b_up[1]])
    every = gather_over_dp((mine + swap(yours)).astype(BF16)).astype(F32)
    shared_size = shared.shape[1]
    shared_far = swap(every[:, :shared_size].astype(BF16)).astype(F32)
    shared_all = jnp.concatenate(
        [
            jnp.where(core == 0, every[:, :shared_size], shared_far),
            jnp.where(core == 0, shared_far, every[:, :shared_size]),
        ],
        axis=1,
    )
    mod_width = 6 * width
    grad_mod_all = shared_all[:, :mod_width]
    small_total = jnp.sum(every[:, shared_size:], axis=0)
    shared_total = jnp.sum(shared_all, axis=0)
    grad_w_mod = jnp.einsum(
        "nt,nm->tm", embed_part.astype(F32), grad_mod_all, precision=lax.Precision.HIGHEST
    )
    embed_terms = jnp.einsum(
        "nm,tm->nt", grad_mod_all, w_mod.astype(F32), precision=lax.Precision.HIGHEST
    )
    grad_temb = lax.all_to_all(embed_terms, "dp", split_axis=0, concat_axis=1, tiled=True)
    return (
        output[None],
        grad_tokens[None],
        grad_temb,
        grad_w_mod,
        shared_total[:mod_width],
        shared_total[mod_width : mod_width + width],
        qkv_total,
        small_total[:qkv_size].reshape(3, half_width),
        out_total,
        shared_total[mod_width + width : mod_width + 2 * width],
        up_total.astype(F32),
        small_total[qkv_size:],
        down_total.astype(F32),
        shared_total[mod_width + 2 * width : mod_width + 3 * width],
    )


def solution(mesh):
    return jax.shard_map(
        shards,
        mesh=mesh,
        in_specs=(
            P("dp", "tensor", None),
            P("dp", None),
            P("dp"),
            P("dp", None),
            P(),
            P(),
            P(None, None, "tensor"),
            P(None, "tensor"),
            P("tensor", None),
            P(),
            P(None, "tensor"),
            P("tensor"),
            P("tensor", None),
            P(),
            P("dp", "tensor", None),
        ),
        out_specs=(
            P("dp", "tensor", None),
            P("dp", "tensor", None),
            P("dp", None),
            P("dp", None),
            P(),
            P(),
            P(None, None, "tensor"),
            P(None, "tensor"),
            P("tensor", None),
            P(),
            P(None, "tensor"),
            P("tensor"),
            P("tensor", None),
            P(),
        ),
        check_vma=False,
    )
```

```python
from math import log, pi, sqrt

import jax
import jax.numpy as jnp
from jax import lax
from jax.experimental import pallas as pl
from jax.experimental.pallas import tpu as pltpu
from jax.sharding import PartitionSpec as P

HEAD_DIM = 64
PAIR = 2 * HEAD_DIM
F32 = jnp.float32
BF16 = jnp.bfloat16
NN = ((1,), (0,))
NT = ((1,), (1,))
TN = ((0,), (0,))
SAFE = 90.0
LN2 = log(2.0)
MIB = 1024 * 1024
VM = pl.BlockSpec(memory_space=pltpu.VMEM)
SM = pl.BlockSpec(memory_space=pltpu.SMEM)


def dot(left, right, dims=NN):
    return lax.dot_general(left, right, (dims, ((), ())), preferred_element_type=F32)


def call(
    body, grid, in_specs, out_specs, out_shape, args, scratch=(), flops=0, moved=0, deps=(), room=6, aliases=None
):
    count = len(in_specs)
    extra = len(deps)
    args = [
        near_core(arg) if spec is VM and arg.size >= 1 << 16 else arg for spec, arg in zip(in_specs, args)
    ]

    def wrapped(*refs):
        body(*refs[:count], *refs[count + extra :])

    return pl.pallas_call(
        wrapped,
        grid=grid,
        in_specs=list(in_specs) + [pl.BlockSpec(memory_space=pl.ANY)] * extra,
        out_specs=out_specs,
        out_shape=out_shape,
        scratch_shapes=list(scratch),
        input_output_aliases=aliases or {},
        compiler_params=pltpu.CompilerParams(
            vmem_limit_bytes=room * MIB, dimension_semantics=("arbitrary",) * len(grid)
        ),
        cost_estimate=pl.CostEstimate(flops=0, bytes_accessed=0, transcendentals=0),
    )(*args, *deps)


def whole(shape):
    return pl.BlockSpec(shape, lambda *_: (0,) * len(shape))


def shape_of(shape, kind):
    return pltpu.VMEM(shape, kind)


def near_core(value):
    return pltpu.with_memory_space_constraint(value, pltpu.VMEM)


def far_core(value):
    return pltpu.with_memory_space_constraint(value, pltpu.HBM)


def norm_parts(field):
    centred = field - jnp.mean(field, axis=-1, keepdims=True)
    inverse = lax.rsqrt(jnp.mean(centred * centred, axis=-1, keepdims=True) + 1e-05)
    return (centred * inverse, inverse)


def norm_back(upstream, normed, inverse):
    return inverse * (
        upstream
        - jnp.mean(upstream, axis=-1, keepdims=True)
        - normed * jnp.mean(upstream * normed, axis=-1, keepdims=True)
    )


def gelu_parts(hidden):
    scale = sqrt(2.0 / pi)
    square = hidden * hidden
    bent = jnp.tanh(hidden * (scale + (scale * 0.044715) * square))
    upper = 0.5 + 0.5 * bent
    slope = upper + (hidden * (0.5 - 0.5 * bent * bent)) * (scale + (3 * 0.044715 * scale) * square)
    return (hidden * upper, slope)


def turn_lanes(field):
    lane = lax.broadcasted_iota(jnp.int32, field.shape, 1)
    up = pltpu.roll(field, PAIR - HEAD_DIM // 2, 1)
    down = pltpu.roll(field, HEAD_DIM // 2, 1)
    return jnp.where((lane & (HEAD_DIM - 1)) < HEAD_DIM // 2, up, down)


def zero_other(field, h, axis):
    place = lax.broadcasted_iota(jnp.int32, field.shape, axis)
    return jnp.where((place >= HEAD_DIM) == (h == 1), field, jnp.zeros_like(field))


def total(field):
    return jnp.sum(field, axis=0, keepdims=True)


def both(near, far):
    return jnp.concatenate([near[...], far[...]], axis=0)


def project_call(near, far, weight, bias, cosine, sine):
    rows, width = near.shape
    half = weight.shape[2]

    def body(xn, xf, w, b, cos, sin, out):
        for i, x in enumerate((xn, xf)):
            here = slice(i * rows, (i + 1) * rows)
            for c in range(3):
                y = dot(x[...], w[c]) + b[c]
                if c == 2:
                    out[c, here] = y.astype(BF16)
                    continue
                for j in range(half // PAIR):
                    of = slice(j * PAIR, (j + 1) * PAIR)
                    u = y[:, of]
                    u = u * cos[here] + turn_lanes(u) * sin[here]
                    if c == 0:
                        u = u * (HEAD_DIM ** (-0.5) / LN2)
                    out[c, here, of] = u.astype(BF16)

    return call(
        body,
        (),
        [VM] * 6,
        VM,
        shape_of((3, 2 * rows, half), BF16),
        (near, far, weight, bias, cosine, sine),
        room=8,
    )


def attend_call(counts, qkv, weight):
    _, keys, half = qkv.shape
    rows = keys // 2
    pairs = half // PAIR
    width = weight.shape[1]

    def body(cnt, q_in, k_in, v_in, w, e_out, ot_out, inv_out, near_out, far_out, o_all):
        j = pl.program_id(0)
        k = k_in[0]
        v_t = v_in[0].T
        near_count, far_count = cnt[0], cnt[1]

        def run(masked, plain):
            for p in range(2):
                of = slice(p * rows, (p + 1) * rows)
                q_t = q_in[0, of].T
                for h in range(2):
                    hs = slice(h * HEAD_DIM, (h + 1) * HEAD_DIM)
                    s = dot(k, zero_other(q_t, h, 0))
                    if masked:
                        place = lax.broadcasted_iota(jnp.int32, (keys, rows), 0)
                        limit = jnp.where(place < rows, near_count, rows + far_count)
                        s = jnp.where(place < limit, s, -1e30)
                    if not plain:
                        s = s - jnp.max(s, axis=0, keepdims=True)
                    e = jnp.exp2(s)
                    inv = 1.0 / total(e)
                    e = e.astype(BF16)
                    e_out[0, h, p] = e
                    inv_out[0, h, :, of] = inv
                    ot_out[hs, of] = (dot(v_t[hs], e) * inv).astype(BF16)

        def norms(field):
            square = field.astype(F32) * field.astype(F32)
            return [
                jnp.max(jnp.sum(zero_other(square, h, 1), axis=1, keepdims=True)) for h in range(2)
            ]

        bound = 0.0
        for one, two in zip(norms(q_in[0]), norms(k)):
            bound = jnp.maximum(bound, one * two)
        plain = bound < SAFE * SAFE
        everything = near_count + far_count >= keys
        pl.when(plain & everything)(lambda: run(False, True))
        pl.when(plain & jnp.logical_not(everything))(lambda: run(True, True))
        pl.when(jnp.logical_not(plain))(lambda: run(True, False))
        o_all[j] = ot_out[...].T

        @pl.when(j == pairs - 1)
        def _():
            o = jnp.concatenate([o_all[i] for i in range(pairs)], axis=1)
            near_out[...] = dot(o[:rows], w[...])
            far_out[...] = dot(o[rows:], w[...]).astype(BF16)

    pick_pair = lambda c: pl.BlockSpec((1, keys, PAIR), lambda j: (c, 0, j))
    return call(
        body,
        (pairs,),
        [SM, pick_pair(0), pick_pair(1), pick_pair(2), whole((half, width))],
        [
            pl.BlockSpec((1, 2, 2, keys, rows), lambda j: (j, 0, 0, 0, 0)),
            pl.BlockSpec((PAIR, keys), lambda j: (j, 0)),
            pl.BlockSpec((1, 2, 1, keys), lambda j: (j, 0, 0, 0)),
            whole((rows, width)),
            whole((rows, width)),
        ],
        [
            pltpu.HBM((pairs, 2, 2, keys, rows), BF16),
            shape_of((half, keys), BF16),
            shape_of((pairs, 2, 1, keys), F32),
            shape_of((rows, width), F32),
            shape_of((rows, width), BF16),
        ],
        (counts, qkv, qkv, qkv, weight),
        [pltpu.VMEM((pairs, keys, PAIR), BF16)],
        flops=16 * keys * keys * half,
        moved=2 * keys * keys * half // HEAD_DIM,
        room=20,
    )


def middle_call(tokens, near, far, vecs):
    rows, width = tokens.shape

    def body(tok, nr, fr, vec, branch_out, fed_out):
        branch = nr[...] + fr[...].astype(F32)
        branch_out[...] = branch
        normed, _ = norm_parts(tok[...].astype(F32) + vec[2:3] * branch)
        fed_out[...] = (normed * vec[3:4] + vec[4:5]).astype(BF16)

    return call(
        body,
        (),
        [VM] * 4,
        [VM] * 2,
        [shape_of((rows, width), F32), shape_of((rows, width), BF16)],
        (tokens, near, far, vecs),
        moved=12 * rows * width,
    )


def mlp_call(first, units, bits, fed, far, g, g_far, up, down, bias, deps=()):
    rows, width = fed.shape
    tile = 256

    def body(bit, fed_in, far_in, g_in, gf_in, up_in, down_in, b_in, send, keep, act_out, dh_out, sums):
        def step(n, carry):
            here = pl.ds(pl.multiple_of(n * tile, tile), tile)
            there = pl.ds(pl.multiple_of(first + n * tile, tile), tile)
            up_w, down_w = up_in[:, there], down_in[there]
            for i, (x, gr) in enumerate(((fed_in, g_in), (far_in, gf_in))):
                of = slice(i * rows, (i + 1) * rows)
                active, slope = gelu_parts(dot(x[...], up_w) + b_in[:, there])
                act_out[of, here] = active.astype(BF16)
                dh_out[of, here] = (dot(gr[...], down_w, NT) * slope).astype(BF16)
            d_hidden = dh_out[:, here]
            down_part = dot(act_out[:, here], both(g_in, gf_in), TN).astype(BF16)
            up_part = dot(both(fed_in, far_in), d_hidden, TN).astype(BF16)
            sums[:, here] = total(d_hidden.astype(F32))

            @pl.when(bit[0] == 0)
            def _():
                keep[here, :] = down_part
                send[:, here] = up_part

            @pl.when(bit[0] != 0)
            def _():
                send[here, :] = down_part
                keep[:, here] = up_part

            return carry

        lax.fori_loop(0, units // tile, step, 0)

    return call(
        body,
        (),
        [SM] + [VM] * 7,
        [VM] * 5,
        [shape_of((width, units), BF16)] * 2
        + [shape_of((2 * rows, units), BF16)] * 2
        + [shape_of((1, units), F32)],
        (bits, fed, far, g, g_far, up, down, bias),
        deps=deps,
        room=12,
    )


def terms_call(parts, weight, dims, deps=()):
    keys, units = parts[0].shape
    rows = keys // 2
    width = weight.shape[0] if dims is NT else weight.shape[1]

    def body(*refs):
        ins, w, near, far = refs[:-3], refs[-3], refs[-2], refs[-1]
        for i, out in enumerate((near, far)):
            acc = 0.0
            for n, part in enumerate(ins):
                of = slice(n * units, (n + 1) * units)
                piece = w[:, of] if dims is NT else w[of]
                acc = acc + dot(part[i * rows : (i + 1) * rows], piece, dims)
            out[...] = acc.astype(out.dtype)

    return call(
        body,
        (),
        [VM] * (len(parts) + 1),
        [VM] * 2,
        [shape_of((rows, width), F32), shape_of((rows, width), BF16)],
        (*parts, weight),
        flops=2 * keys * width * units * len(parts),
        moved=8 * keys * width,
        deps=deps,
        room=8,
    )


def input_call(normed, vecs):
    rows, width = normed.shape

    def body(n, vec, out):
        out[...] = (n[...] * vec[0:1] + vec[1:2]).astype(BF16)

    return call(body, (), [VM, VM], VM, shape_of((rows, width), BF16), (normed, vecs))


def masked(cnt, field):
    place = lax.broadcasted_iota(jnp.int32, field.shape, 0)
    return jnp.where(place < cnt[0], field.astype(F32), 0.0)


def upstream_call(counts, cotangent, vecs):
    rows, width = cotangent.shape

    def body(cnt, cot, vec, g_out, sum_out):
        g = (masked(cnt, cot[...]) * vec[5:6]).astype(BF16)
        g_out[...] = g
        sum_out[...] = total(g.astype(F32))

    return call(
        body,
        (),
        [SM, VM, VM],
        [VM, VM],
        [shape_of((rows, width), BF16), shape_of((1, width), F32)],
        (counts, cotangent, vecs),
    )


def turn_call(counts, tokens, cotangent, branch, d_near, d_far, vecs, deps=()):
    rows, width = tokens.shape

    def body(cnt, tok, cot, br, dn, df, vec, dm_out, g_out, sum_out):
        normed, inverse = norm_parts(tok[...].astype(F32) + vec[2:3] * br[...])
        d_in = dn[...] + df[...].astype(F32)
        d_middle = masked(cnt, cot[...]) + norm_back(d_in * vec[3:4], normed, inverse)
        g_out[...] = (d_middle * vec[2:3]).astype(BF16)
        dm_out[...] = d_middle
        sum_out[0:1] = total(d_middle * br[...])
        sum_out[1:2] = total(d_in)
        sum_out[2:3] = total(d_in * normed)
        sum_out[3:8] = jnp.zeros((5, width), F32)

    return call(
        body,
        (),
        [SM] + [VM] * 6,
        [VM] * 3,
        [shape_of((rows, width), F32), shape_of((rows, width), BF16), shape_of((8, width), F32)],
        (counts, tokens, cotangent, branch, d_near, d_far, vecs),
        deps=deps,
    )


def finish_call(counts, tokens, cotangent, branch, b_near, b_far, vecs, deps=()):
    rows, width = tokens.shape

    def body(cnt, tok, cot, br, bn, bf, vec, y_out, sum_out):
        middle = tok[...].astype(F32) + vec[2:3] * br[...]
        mlp_branch = bn[...] + bf[...].astype(F32) + vec[6:7]
        y_out[...] = masked(cnt, middle + vec[5:6] * mlp_branch).astype(BF16)
        sum_out[0:1] = total(masked(cnt, cot[...]) * mlp_branch)
        sum_out[1:8] = jnp.zeros((7, width), F32)

    return call(
        body,
        (),
        [SM] + [VM] * 6,
        [VM] * 2,
        [pltpu.HBM((rows, width), BF16), shape_of((8, width), F32)],
        (counts, tokens, cotangent, branch, b_near, b_far, vecs),
        deps=deps,
    )


def turn_out_call(near, far, weight, o_t, deps=()):
    rows, width = near.shape
    half = weight.shape[0]

    def body(gn, gf, w, ot, d_out, w_out):
        g = jnp.concatenate([gn[...], gf[...]], axis=0)
        d_out[...] = dot(w[...], g, NT).astype(BF16)
        grad = dot(ot[...], g).astype(BF16)
        w_out[0:half] = grad[:, :half]
        w_out[half:] = grad[:, half:]

    return call(
        body,
        (),
        [VM] * 4,
        [VM] * 2,
        [shape_of((half, 2 * rows), BF16), shape_of((width, half), BF16)],
        (near, far, weight, o_t),
        flops=8 * rows * width * half,
        moved=6 * rows * width,
        deps=deps,
    )


def attend_back_call(j, qkv, e, o_t, inv, d_t, cosine, sine, near, far, deps=()):
    _, keys, half = qkv.shape
    rows = keys // 2
    width = near.shape[1]
    quarter = HEAD_DIM // 2

    def body(qkv_in, e_hbm, ot_all, inv_in, d_all, cos, sin, xn, xf, grad_out, d_out, sums, e_in, sems):
        lanes = slice(j * PAIR, (j + 1) * PAIR)
        ot_in, d_in = ot_all.at[lanes], d_all.at[lanes]

        def copy(p, h):
            n = 2 * p + h
            return pltpu.make_async_copy(e_hbm.at[j, h, p], e_in.at[n], sems.at[n])

        for p in range(2):
            for h in range(2):
                copy(p, h).start()
        k_t = qkv_in[1, :, lanes].T
        v = qkv_in[2, :, lanes]
        cos_t = cos[...].T[:quarter]
        sin_t = sin[...].T[quarter : 2 * quarter]
        d_k = d_v = 0.0
        d_q = []
        for p in range(2):
            of = slice(p * rows, (p + 1) * rows)
            scaled = []
            for h in range(2):
                hs = slice(h * HEAD_DIM, (h + 1) * HEAD_DIM)
                scaled.append((d_in[hs, of].astype(F32) * inv_in[j, h, :, of]).astype(BF16))
            d_t = jnp.concatenate(scaled, axis=0)
            d = d_t.T
            q = qkv_in[0, of, lanes]
            turned = []
            for h in range(2):
                hs = slice(h * HEAD_DIM, (h + 1) * HEAD_DIM)
                delta = total(d_t[hs].astype(F32) * ot_in[hs, of].astype(F32))
                d_p = dot(v, zero_other(d_t, h, 0))
                copy(p, h).wait()
                weight = e_in[2 * p + h]
                d_s = (weight.astype(F32) * (d_p - delta)).astype(BF16)
                d_v = d_v + dot(weight, zero_other(d, h, 1))
                d_k = d_k + dot(d_s, zero_other(q, h, 1))
                t = dot(k_t[hs], d_s) * HEAD_DIM ** (-0.5)
                one, two = t[:quarter], t[quarter:]
                turned.append((one * cos_t[:, of] + two * sin_t[:, of]).astype(BF16))
                turned.append((two * cos_t[:, of] - one * sin_t[:, of]).astype(BF16))
            d_q.append(jnp.concatenate(turned, axis=0).T)
        u = d_k * LN2
        d_k = (u * cos[...] - turn_lanes(u) * sin[...]).astype(BF16)
        every = jnp.concatenate([jnp.concatenate(d_q, axis=0), d_k, d_v.astype(BF16)], axis=1)
        d_out[...] = every
        grad_out[...] = dot(both(xn, xf), every, TN).astype(BF16)
        sums[...] = total(every.astype(F32))

    return call(
        body,
        (),
        [VM, pl.BlockSpec(memory_space=pltpu.HBM)] + [VM] * 7,
        [VM] * 3,
        [
            shape_of((width, 3 * PAIR), BF16),
            shape_of((keys, 3 * PAIR), BF16),
            shape_of((1, 3 * PAIR), F32),
        ],
        (qkv, far_core(e), o_t, inv, d_t, cosine, sine, near, far),
        [pltpu.VMEM((4, keys, rows), BF16), pltpu.SemaphoreType.DMA((4,))],
        flops=32 * keys * keys * PAIR,
        moved=4 * keys * keys,
        deps=deps,
        room=14,
    )


def input_terms_call(parts, weight, deps=()):
    keys = parts[0].shape[0]
    rows = keys // 2
    _, width, half = weight.shape

    def body(*refs):
        ins, w, near, far = refs[:-3], refs[-3], refs[-2], refs[-1]
        for i, out in enumerate((near, far)):
            acc = 0.0
            for c in range(3):
                of = slice(c * PAIR, (c + 1) * PAIR)
                d = jnp.concatenate([part[i * rows : (i + 1) * rows, of] for part in ins], axis=1)
                acc = acc + dot(d, w[c], NT)
            out[...] = acc.astype(out.dtype)

    return call(
        body,
        (),
        [VM] * (len(parts) + 1),
        [VM] * 2,
        [shape_of((rows, width), F32), shape_of((rows, width), BF16)],
        (*parts, weight),
        flops=6 * keys * width * half,
        moved=8 * keys * width,
        deps=deps,
        room=8,
    )


def end_call(tokens, d_middle, near, far, vecs, deps=()):
    rows, width = tokens.shape

    def body(tok, dm, dn, df, vec, grad_out, sum_out):
        normed, inverse = norm_parts(tok[...].astype(F32))
        d_in = dn[...] + df[...].astype(F32)
        grad_out[...] = (dm[...] + norm_back(d_in * vec[0:1], normed, inverse)).astype(BF16)
        sum_out[0:1] = total(d_in)
        sum_out[1:2] = total(d_in * normed)
        sum_out[2:8] = jnp.zeros((6, width), F32)

    return call(
        body,
        (),
        [VM] * 5,
        [VM] * 2,
        [pltpu.HBM((rows, width), BF16), shape_of((8, width), F32)],
        (tokens, d_middle, near, far, vecs),
        moved=16 * rows * width,
        deps=deps,
    )


def swap(value):
    return lax.ppermute(value, "tensor", [(0, 1), (1, 0)])


def bit_swap(value, bit, order_by_core):
    pairs = []
    for place in range(lax.axis_size("dp")):
        for core in range(2):
            use = bit ^ core if order_by_core else bit
            pairs.append((place * 2 + core, (place ^ (1 << use)) * 2 + core))
    return lax.ppermute(value, ("dp", "tensor"), pairs)


def pick(value, index):
    return lax.dynamic_index_in_dim(value, index, 0, keepdims=False)


def join(mine, other, index):
    return jnp.where(index == 0, jnp.stack([mine, other]), jnp.stack([other, mine]))


def bit_count():
    return lax.axis_size("dp").bit_length() - 1


def pack_call(blocks, bit, deps=()):
    width, size = blocks[0].shape

    def body(b, one, two, three, four, send, keep):
        def put(low, high):
            low[:, :size], low[:, size:] = one[...], two[...]
            high[:, :size], high[:, size:] = three[...], four[...]

        pl.when(b[0] == 0)(lambda: put(keep, send))
        pl.when(b[0] != 0)(lambda: put(send, keep))

    return call(
        body,
        (),
        [SM] + [VM] * 4,
        [VM, VM],
        [shape_of((width, 2 * size), BF16)] * 2,
        (bit, *blocks),
        deps=deps,
    )


def shared_call(end_sums, turn_sums, out_sums, down_sums, vecs, deps=()):
    width = vecs.shape[1]

    def body(ends, turn, out, down, vec, rows):
        rows[0:1] = ends[0:1]
        rows[1:2] = ends[1:2] * vec[7:8]
        rows[2:4] = turn[0:2]
        rows[4:5] = turn[2:3] * vec[8:9]
        rows[5:6] = out[0:1]
        rows[6:7] = ends[1:2] * vec[9:10]
        rows[7:8] = turn[2:3] * vec[10:11]
        rows[8:9] = down[...]
        rows[9:16] = jnp.zeros((7, width), F32)

    return call(
        body,
        (),
        [VM] * 5,
        VM,
        shape_of((16, width), F32),
        (end_sums, turn_sums, out_sums, down_sums, vecs),
        deps=deps,
    )


def small_call(mine, other, b_up_sums, b_qkv_sums, deps=()):
    width = mine.shape[1]
    half = width // 2

    def body(one, two, up_0, up_1, qkv_0, qkv_1, qkv_2, rows):
        rows[0:16] = (one[...] + two[...]).astype(BF16)
        extra = jnp.concatenate(
            [
                up_0[...],
                up_1[...],
                jnp.concatenate([qkv_0[...], qkv_1[...]], axis=1),
                jnp.concatenate([qkv_2[...], jnp.zeros((1, half), F32)], axis=1),
                jnp.zeros((12, width), F32),
            ],
            axis=0,
        )
        rows[16:32] = extra.astype(BF16)

    return call(
        body,
        (),
        [VM] * 7,
        VM,
        shape_of((32, width), BF16),
        (mine, other, *b_up_sums, *b_qkv_sums),
        deps=deps,
    )


def append_call(mine, other, deps=()):
    rows, width = mine.shape

    def body(one, two, out):
        out[:rows] = one[...]
        out[rows:] = two[...]

    return call(
        body, (), [VM, VM], VM, shape_of((2 * rows, width), BF16), (mine, other), deps=deps
    )


def split_add(mine, other, bit, deps=()):
    rows, width = mine.shape

    def body(b, one, two, send, keep):
        field = (one[...].astype(F32) + two[...].astype(F32)).astype(BF16)
        low, high = field[: rows // 2], field[rows // 2 :]

        @pl.when(b[0] == 0)
        def _():
            keep[...] = low
            send[...] = high

        @pl.when(b[0] != 0)
        def _():
            send[...] = low
            keep[...] = high

    return call(
        body,
        (),
        [SM, VM, VM],
        [VM, VM],
        [shape_of((rows // 2, width), BF16)] * 2,
        (bit, mine, other),
        moved=6 * rows * width,
        deps=deps,
    )


def plain_add(mine, other, deps=()):
    def body(one, two, out):
        out[...] = (one[...].astype(F32) + two[...].astype(F32)).astype(BF16)

    return call(
        body, (), [VM, VM], VM, shape_of(mine.shape, BF16), (mine, other), moved=6 * mine.size, deps=deps
    )


def stack_halves(mine, other, bit, deps=()):
    rows, width = mine.shape

    def body(b, one, two, out):
        out[pl.ds(pl.multiple_of(b[0] * rows, rows), rows)] = one[...]
        out[pl.ds(pl.multiple_of((1 - b[0]) * rows, rows), rows)] = two[...]

    return call(
        body,
        (),
        [SM, VM, VM],
        VM,
        shape_of((2 * rows, width), BF16),
        (bit, mine, other),
        moved=8 * mine.size,
        deps=deps,
    )


def unpack_call(mine, other, bit, before, units, at, deps=()):
    width = mine.shape[0]
    size = mine.shape[1]

    def body(b, one, two, *rest):
        down_out, up_out = rest[-2:]

        @pl.when(b[0] == 0)
        def _():
            down_out[...] = one[...].astype(F32)
            up_out[...] = two[...].astype(F32)

        @pl.when(b[0] != 0)
        def _():
            down_out[...] = two[...].astype(F32)
            up_out[...] = one[...].astype(F32)

    extra = [pl.BlockSpec(memory_space=pl.ANY)] * len(before)
    return call(
        body,
        (1,),
        [SM, whole(mine.shape), whole(mine.shape)] + extra,
        [
            pl.BlockSpec((size, width), lambda i: (at, 0)),
            pl.BlockSpec((width, size), lambda i: (0, at)),
        ],
        [pltpu.HBM((units, width), F32), pltpu.HBM((width, units), F32)],
        (bit, mine, other) + tuple(far_core(x) for x in before),
        moved=12 * mine.size,
        deps=deps,
        aliases={3: 0, 4: 1} if before else None,
        room=16,
    )


def unpack_last_call(mine, other, bit, deps=()):
    width, size = mine.shape
    half = size // 2

    def body(b, one, two, qkv_out, out_out):
        def put(low, high):
            for j, block in enumerate((low[:, :half], low[:, half:], high[:, :half])):
                for c in range(3):
                    qkv_out[c, :, j * PAIR : (j + 1) * PAIR] = block[:, c * PAIR : (c + 1) * PAIR].astype(F32)
            out_out[:, :half] = high[:half, half:].astype(F32)
            out_out[:, half:] = high[half:, half:].astype(F32)

        pl.when(b[0] == 0)(lambda: put(one, two))
        pl.when(b[0] != 0)(lambda: put(two, one))

    return call(
        body,
        (),
        [SM, VM, VM],
        [VM, VM],
        [pltpu.HBM((3, width, half), F32), pltpu.HBM((half, width), F32)],
        (bit, mine, other),
        moved=12 * mine.size,
        deps=deps,
    )


def reduce_steps(send, keep, bits, halve):
    first, second, third = bits
    other = bit_swap(send, 0, True)
    deps = yield other
    send, keep = split_add(keep, other, second, deps)
    other = bit_swap(send, 1, True)
    deps = yield send, other
    if halve:
        send, keep = split_add(keep, other, third, deps)
        other = bit_swap(send, 2, False)
        deps = yield send, other
        mine = plain_add(keep, other, deps)
    else:
        mine = plain_add(keep, other, deps)
        other = bit_swap(mine, 2, False)
        deps = yield mine, other
        mine = plain_add(mine, other, deps)
    for bit in range(3, bit_count()):
        other = bit_swap(mine, bit, False)
        deps = yield mine, other
        mine = plain_add(mine, other, deps)
    if halve:
        other = bit_swap(mine, 2, False)
        deps = yield mine, other
        mine = stack_halves(mine, other, third, deps)
    other = bit_swap(mine, 1, True)
    deps = yield mine, other
    mine = stack_halves(mine, other, second, deps)
    yield mine, (mine, bit_swap(mine, 0, True))


class Gather:
    def __init__(self, value, line):
        self.line = line
        self.value = value
        self.bit = 0
        self.other = bit_swap(value, 0, False)

    def go(self):
        if self.bit < bit_count():
            self.value = append_call(self.value, self.other, self.line.last)
            self.line.after(self.value)
            self.bit += 1
            if self.bit < bit_count():
                self.other = bit_swap(self.value, self.bit, False)

    def all(self):
        while self.bit < bit_count():
            self.go()
        return self.value


def tree_sum(value):
    while value.shape[0] > 1:
        value = value.reshape((-1, 2) + value.shape[1:])
        value = value[:, 0] + value[:, 1]
    return value[0]


class Line:
    def __init__(self):
        self.last = ()

    def after(self, value):
        self.last = (value,)


class Group:
    def __init__(self, name, send, keep, bits, line, halve=True):
        self.line = line
        self.name = name
        self.steps = reduce_steps(send, keep, bits, halve)
        self.done = False
        with jax.named_scope(name):
            self.waiting = next(self.steps)

    def go(self):
        if not self.done:
            with jax.named_scope(self.name):
                mine, self.waiting = self.steps.send(self.line.last)
            self.line.after(mine)
            self.done = isinstance(self.waiting, tuple)

    def halves(self):
        while not self.done:
            self.go()
        return self.waiting


def shards(
    tokens,
    temb,
    lengths,
    w_mod,
    b_mod,
    gain_attn,
    query_key_value_weight,
    b_qkv,
    attention_output_weight,
    gain_mlp,
    up_weight,
    b_up,
    down_weight,
    b_down,
    cotangent,
):
    tokens, cotangent, length = tokens[0], cotangent[0], lengths[0]
    rows, width = tokens.shape
    core = lax.axis_index("tensor")
    place = lax.axis_index("dp")
    bits = [
        jnp.reshape((place >> b) & 1, (1,)).astype(jnp.int32) for b in (core, 1 - core, jnp.int32(2))
    ]
    half = width // 2
    start = core * rows
    counts = jnp.clip(jnp.stack([length - start, length - (rows - start)]), 0, rows)

    qkv_weight = jnp.swapaxes(query_key_value_weight, 0, 1)
    qkv_bias = b_qkv.reshape(3, 1, half).astype(F32)
    up_bias = b_up.reshape(1, -1).astype(F32)
    quarter = HEAD_DIM // 2
    lane = lax.iota(jnp.int32, PAIR)
    frequency = 10000.0 ** (-(lane & (quarter - 1)).astype(F32) / quarter)
    sign = jnp.where((lane & quarter) == 0, -1.0, 1.0)
    order = lax.iota(jnp.int32, rows)
    places = jnp.concatenate([start + order, (rows - start) + order]).astype(F32)
    angles = places[:, None] * frequency[None, :]
    cosine, sine = jnp.cos(angles), jnp.sin(angles) * sign[None, :]
    normed_attn, _ = norm_parts(tokens.astype(F32))

    embed_part = lax.all_to_all(temb, "dp", split_axis=1, concat_axis=0, tiled=True)
    mod_terms = jnp.dot(embed_part, w_mod, preferred_element_type=F32)
    mod_terms = lax.all_to_all(mod_terms, "dp", split_axis=0, concat_axis=0, tiled=True)
    mod_terms, cosine, sine, normed_attn, qkv_bias, up_bias = lax.optimization_barrier(
        (mod_terms, cosine, sine, normed_attn, qkv_bias, up_bias)
    )
    modulation = jnp.sum(mod_terms, axis=0) + b_mod.astype(F32)
    shift_attn, scale_attn, gate_attn, shift_mlp, scale_mlp, gate_mlp = modulation.reshape(6, width)
    gain_attn = gain_attn.astype(F32)
    gain_mlp = gain_mlp.astype(F32)
    vecs = jnp.stack(
        [
            gain_attn * (1.0 + scale_attn),
            shift_attn,
            gate_attn,
            gain_mlp * (1.0 + scale_mlp),
            shift_mlp,
            gate_mlp,
            b_down.astype(F32),
            gain_attn,
            gain_mlp,
            1.0 + scale_attn,
            1.0 + scale_mlp,
        ]
    )

    attn_in = input_call(normed_attn, vecs)
    attn_in_far = swap(attn_in)
    qkv = project_call(attn_in, attn_in_far, qkv_weight, qkv_bias, cosine, sine)
    g_mlp, down_sums = upstream_call(counts, cotangent, vecs)
    g_mlp_far = swap(g_mlp)
    e, o_t, inv, branch_near, branch_far = attend_call(counts, qkv, attention_output_weight)
    attn_branch, fed = middle_call(tokens, branch_near, swap(branch_far), vecs)
    fed_far = swap(fed)
    units = up_weight.shape[1]
    size = units // 2
    line = Line()
    actives, d_hiddens, b_up_sums, groups = [], [], [], []
    for part in range(2):
        send, keep, active, d_hidden, b_up_sum = mlp_call(
            part * size, size, bits[0], fed, fed_far, g_mlp, g_mlp_far, up_weight, down_weight, up_bias, line.last
        )
        line.after(send)
        groups.append(Group(("mlp_first", "mlp_second")[part], send, keep, bits, line))
        actives.append(active)
        d_hiddens.append(d_hidden)
        b_up_sums.append(b_up_sum)
    one, two = groups
    d_near, d_far = terms_call(d_hiddens, up_weight, NT, line.last)
    line.after(d_far)
    b_near, b_far = terms_call(actives, down_weight, NN, line.last)
    line.after(b_far)
    d_middle, g_attn, turn_sums = turn_call(
        counts, tokens, cotangent, attn_branch, d_near, swap(d_far), vecs, line.last
    )
    line.after(g_attn)
    b_swapped = swap(b_far)
    g_attn_far = swap(g_attn)
    one.go()
    d_t, grad_out = turn_out_call(g_attn, g_attn_far, attention_output_weight, o_t, line.last)
    line.after(d_t)
    grads, d_alls, b_qkv_sums = [], [], []
    for j in range(half // PAIR):
        grad, d_all, b_qkv_sum = attend_back_call(
            j, qkv, e, o_t, inv, d_t, cosine, sine, attn_in, attn_in_far, line.last
        )
        line.after(grad)
        grads.append(grad)
        d_alls.append(d_all)
        b_qkv_sums.append(b_qkv_sum)
        if j < 2:
            two.go()
            one.go()
    send, keep = pack_call(grads + [grad_out], bits[0], line.last)
    line.after(send)
    three = Group("projections", send, keep, bits, line)
    d_near, d_far = input_terms_call(d_alls, qkv_weight, line.last)
    line.after(d_far)
    output, out_sums = finish_call(
        counts, tokens, cotangent, attn_branch, b_near, b_swapped, vecs, line.last
    )
    line.after(output)
    two.go()
    one.go()
    three.go()
    grad_tokens, end_sums = end_call(tokens, d_middle, d_near, swap(d_far), vecs, line.last)
    line.after(grad_tokens)
    shared = shared_call(end_sums, turn_sums, out_sums, down_sums, vecs, line.last)
    line.after(shared)
    shared_far = swap(shared)
    two.go()
    one.go()
    three.go()
    small = small_call(shared, shared_far, b_up_sums, b_qkv_sums, line.last)
    line.after(small)
    gather = Gather(small, line)
    two.go()
    one.go()
    three.go()
    gather.go()
    two.go()
    three.go()
    gather.go()
    totals = unpack_call(*one.halves(), bits[0], (), units, 0, line.last)
    line.after(totals[0])
    three.go()
    gather.go()
    totals = unpack_call(*two.halves(), bits[0], totals, units, 1, line.last)
    line.after(totals[0])
    three.go()
    every = gather.all().reshape(-1, 32, width)
    grad_mod_all = every[:, :6].reshape(-1, 6 * width)
    embed_order = lax.iota(jnp.int32, every.shape[0]) ^ place
    embed_here = jnp.take(embed_part, embed_order, axis=0)
    grad_w_mod = dot(embed_here, grad_mod_all, TN)
    embed_terms = jnp.take(dot(grad_mod_all, w_mod, NT), embed_order, axis=0)
    grad_temb = lax.all_to_all(embed_terms, "dp", split_axis=0, concat_axis=1, tiled=True)
    sums = tree_sum(every.astype(F32))

    down_total, up_total = totals
    qkv_total, out_total = unpack_last_call(*three.halves(), bits[0], line.last)
    b_up_total = sums[16:18].reshape(-1)
    b_qkv_total = sums[18:20].reshape(-1)[: 9 * PAIR].reshape(3, 3, PAIR)
    return (
        output[None],
        grad_tokens[None],
        grad_temb,
        grad_w_mod,
        sums[:6].reshape(-1),
        sums[6],
        jnp.swapaxes(qkv_total, 0, 1),
        jnp.swapaxes(b_qkv_total, 0, 1).reshape(3, half),
        out_total,
        sums[7],
        up_total,
        b_up_total,
        down_total,
        sums[8],
    )


def solution(mesh):
    return jax.shard_map(
        shards,
        mesh=mesh,
        in_specs=(
            P("dp", "tensor", None),
            P("dp", None),
            P("dp"),
            P("dp", None),
            P(),
            P(),
            P(None, None, "tensor"),
            P(None, "tensor"),
            P("tensor", None),
            P(),
            P(None, "tensor"),
            P("tensor"),
            P("tensor", None),
            P(),
            P("dp", "tensor", None),
        ),
        out_specs=(
            P("dp", "tensor", None),
            P("dp", "tensor", None),
            P("dp", None),
            P("dp", None),
            P(),
            P(),
            P(None, None, "tensor"),
            P(None, "tensor"),
            P("tensor", None),
            P(),
            P(None, "tensor"),
            P("tensor"),
            P("tensor", None),
            P(),
        ),
        check_vma=False,
    )
```

```python
from functools import partial
from math import log, pi, sqrt

import jax
import jax.numpy as jnp
from jax import lax
from jax.experimental import pallas as pl
from jax.experimental.pallas import tpu as pltpu
from jax.sharding import PartitionSpec as P

HEAD_DIM = 64
PAIR = 2 * HEAD_DIM
F32 = jnp.float32
BF16 = jnp.bfloat16
NN = ((1,), (0,))
NT = ((1,), (1,))
TN = ((0,), (0,))
SAFE = 90.0
LONG = 10**9
ORDER = (
    "mlp_first", "turn", "back", "mlp_second", "mlp_first", "d_attn_in", "mlp_second", "mlp_first",
    "finish", "end", "share", "mlp_second", "projections", "mlp_first", "projections", "begin",
    "mlp_first", "mlp_second", "projections", "small", "mlp_first", "projections", "small",
    "mlp_second", "unpack_first", "projections", "mlp_second", "small", "small", "projections",
    "unpack_second",
)
LN2 = log(2.0)
MIB = 1024 * 1024
VM = pl.BlockSpec(memory_space=pltpu.VMEM)
SM = pl.BlockSpec(memory_space=pltpu.SMEM)
HB = pl.BlockSpec(memory_space=pltpu.HBM)


def dot(left, right, dims=NN):
    return lax.dot_general(left, right, (dims, ((), ())), preferred_element_type=F32)


class Late:
    def __init__(self, *parts):
        self.parts = parts or ((),)


class Queue:
    def __init__(self, copies, ahead):
        self.copies = copies
        self.started = 0
        self.here = set()
        self.start(ahead)

    def start(self, count):
        for copy in self.copies[self.started : self.started + count]:
            copy.start()
        self.started += count

    def need(self, n):
        if n not in self.here:
            self.start(max(0, n + 1 - self.started))
            self.here.add(n)
            self.copies[n].wait()
            self.start(1)


class LateRef:
    def __init__(self, queue, places, refs):
        self.queue = queue
        self.places = places
        self.refs = refs

    def get(self, n=0):
        self.queue.need(self.places[n])
        return self.refs[n]


def call(body, grid, in_specs, out_specs, out_shape, args, scratch=(), line=None, room=12, aliases=None, ahead=3, rank=None, cost=None):
    count = len(in_specs)
    single = not isinstance(out_shape, list)
    out_specs = [out_specs] if single else list(out_specs)
    out_shape = [out_shape] if single else list(out_shape)
    outs = len(out_shape)
    late = [n for n, spec in enumerate(in_specs) if isinstance(spec, Late)]
    pieces = [(n, part) for n in late for part in in_specs[n].parts]
    if rank is not None:
        pieces.sort(key=lambda piece: rank(piece[0], in_specs[piece[0]].parts.index(piece[1])))
    buffers = [
        pltpu.VMEM(jax.eval_shape(lambda x, part=part: x[part], args[n]).shape, args[n].dtype)
        for n, part in pieces
    ]
    args = [far_core(arg) if n in late else arg for n, arg in enumerate(args)]
    in_specs = [HB if n in late else spec for n, spec in enumerate(in_specs)]
    if pieces:
        buffers.append(pltpu.SemaphoreType.DMA((len(pieces),)))
    extra = 0
    if line is not None:
        extra = 1
        cost = LONG if cost is None else cost
        in_specs.append(pl.BlockSpec(memory_space=pl.ANY))
        args.append(line.turn)
        out_specs.append(VM)
        out_shape.append(shape_of((8, 128), F32))

    def wrapped(*refs):
        ins = list(refs[:count])
        rest = list(refs[count + extra : count + extra + outs])
        if extra:
            refs[count + extra + outs][...] = jnp.zeros((8, 128), F32)
        rest += refs[count + 2 * extra + outs :]
        if pieces:
            rest, held, sems = rest[: -len(buffers)], rest[-len(buffers) : -1], rest[-1]
            copies = []
            for i, (n, part) in enumerate(pieces):
                source = ins[n].at[part] if part else ins[n]
                copies.append(pltpu.make_async_copy(source, held[i], sems.at[i]))
            queue = Queue(copies, ahead)
            for n in late:
                mine = [i for i, (m, _) in enumerate(pieces) if m == n]
                ins[n] = LateRef(queue, mine, [held[i] for i in mine])
        body(*ins, *rest)
        if pieces:
            for i in range(len(pieces)):
                queue.need(i)

    result = pl.pallas_call(
        wrapped,
        grid=grid,
        in_specs=in_specs,
        out_specs=out_specs,
        out_shape=out_shape,
        scratch_shapes=list(scratch) + buffers,
        input_output_aliases=aliases or {},
        compiler_params=pltpu.CompilerParams(
            vmem_limit_bytes=room * MIB, dimension_semantics=("arbitrary",) * len(grid)
        ),
        cost_estimate=pl.CostEstimate(flops=cost or 0, bytes_accessed=0, transcendentals=0),
    )(*args)
    if extra:
        line.turn = result[-1]
        result = result[:-1]
    return result[0] if single else result


def whole(shape):
    return pl.BlockSpec(shape, lambda *_: (0,) * len(shape))


def shape_of(shape, kind):
    return pltpu.VMEM(shape, kind)


def far_core(value):
    return pltpu.with_memory_space_constraint(value, pltpu.HBM)


def norm_parts(field):
    centred = field - jnp.mean(field, axis=-1, keepdims=True)
    inverse = lax.rsqrt(jnp.mean(centred * centred, axis=-1, keepdims=True) + 1e-05)
    return (centred * inverse, inverse)


def norm_back(upstream, normed, inverse):
    return inverse * (
        upstream
        - jnp.mean(upstream, axis=-1, keepdims=True)
        - normed * jnp.mean(upstream * normed, axis=-1, keepdims=True)
    )


def gelu_parts(hidden):
    scale = sqrt(2.0 / pi)
    square = hidden * hidden
    bent = jnp.tanh(hidden * (scale + (scale * 0.044715) * square))
    upper = 0.5 + 0.5 * bent
    slope = upper + (hidden * (0.5 - 0.5 * bent * bent)) * (scale + (3 * 0.044715 * scale) * square)
    return (hidden * upper, slope)


def turn_lanes(field):
    lane = lax.broadcasted_iota(jnp.int32, field.shape, 1)
    up = pltpu.roll(field, PAIR - HEAD_DIM // 2, 1)
    down = pltpu.roll(field, HEAD_DIM // 2, 1)
    return jnp.where((lane & (HEAD_DIM - 1)) < HEAD_DIM // 2, up, down)


def zero_other(field, h, axis):
    place = lax.broadcasted_iota(jnp.int32, field.shape, axis)
    return jnp.where((place >= HEAD_DIM) == (h == 1), field, jnp.zeros_like(field))


def total(field):
    return jnp.sum(field, axis=0, keepdims=True)


def both(near, far):
    return jnp.concatenate([near[...], far[...]], axis=0)


def attend_call(counts, near, far, weight, bias, cosine, sine, out_weight):
    rows, width = near.shape
    keys = 2 * rows
    half = weight.shape[2]
    pairs = half // PAIR
    quarter = HEAD_DIM // 2

    def body(
        cnt, xn, xf, w, b, cos, sin, w_out, e_out, ot_out, inv_out, near_out, far_out, qkv_out, trig, qkv, o_all, sem
    ):
        j = pl.program_id(0)
        store = pltpu.make_async_copy(qkv, qkv_out, sem.at[0])

        @pl.when(j == 0)
        def _():
            for c in range(3):
                for i, x in enumerate((xn, xf)):
                    here = slice(i * rows, (i + 1) * rows)
                    y = dot(x[...], w[c]) + b[c]
                    for n in range(pairs):
                        u = y[:, n * PAIR : (n + 1) * PAIR]
                        if c < 2:
                            u = u * cos[here] + turn_lanes(u) * sin[here]
                        if c == 0:
                            u = u * (HEAD_DIM ** (-0.5) / LN2)
                        qkv[c, n, here] = u.astype(BF16)
            trig[:quarter] = cos[...].T[:quarter]
            trig[quarter:] = sin[...].T[quarter : 2 * quarter]
            store.start()

        q_in = qkv.at[0, j]
        k = qkv[1, j]
        v_t = qkv[2, j].T
        near_count, far_count = cnt[0], cnt[1]

        def run(masked, plain):
            for p in range(2):
                of = slice(p * rows, (p + 1) * rows)
                q_t = q_in[of].T
                for h in range(2):
                    hs = slice(h * HEAD_DIM, (h + 1) * HEAD_DIM)
                    s = dot(k, zero_other(q_t, h, 0))
                    if masked:
                        place = lax.broadcasted_iota(jnp.int32, (keys, rows), 0)
                        limit = jnp.where(place < rows, near_count, rows + far_count)
                        s = jnp.where(place < limit, s, -1e30)
                    if not plain:
                        s = s - jnp.max(s, axis=0, keepdims=True)
                    e = jnp.exp2(s)
                    inv = 1.0 / total(e)
                    e = e.astype(BF16)
                    e_out[0, h, p] = e
                    inv_out[0, h, :, of] = inv
                    ot_out[hs, of] = (dot(v_t[hs], e) * inv).astype(BF16)

        def norms(field):
            square = field.astype(F32) * field.astype(F32)
            return [
                jnp.max(jnp.sum(zero_other(square, h, 1), axis=1, keepdims=True)) for h in range(2)
            ]

        bound = 0.0
        for one, two in zip(norms(q_in[...]), norms(k)):
            bound = jnp.maximum(bound, one * two)
        plain = bound < SAFE * SAFE
        everything = near_count + far_count >= keys
        pl.when(plain & everything)(lambda: run(False, True))
        pl.when(plain & jnp.logical_not(everything))(lambda: run(True, True))
        pl.when(jnp.logical_not(plain))(lambda: run(True, False))
        o_all[j] = ot_out[...].T

        @pl.when(j == pairs - 1)
        def _():
            o = jnp.concatenate([o_all[i] for i in range(pairs)], axis=1)
            near_out[...] = dot(o[:rows], w_out[...])
            far_out[...] = dot(o[rows:], w_out[...]).astype(BF16)
            store.wait()

    return call(
        body,
        (pairs,),
        [
            SM,
            whole((rows, width)),
            whole((rows, width)),
            whole((3, width, half)),
            whole((3, 1, half)),
            whole((keys, PAIR)),
            whole((keys, PAIR)),
            whole((half, width)),
        ],
        [
            pl.BlockSpec((1, 2, 2, keys, rows), lambda j: (j, 0, 0, 0, 0)),
            pl.BlockSpec((PAIR, keys), lambda j: (j, 0)),
            pl.BlockSpec((1, 2, 1, keys), lambda j: (j, 0, 0, 0)),
            whole((rows, width)),
            whole((rows, width)),
            HB,
            whole((HEAD_DIM, keys)),
        ],
        [
            pltpu.HBM((pairs, 2, 2, keys, rows), BF16),
            pltpu.HBM((half, keys), BF16),
            shape_of((pairs, 2, 1, keys), F32),
            shape_of((rows, width), F32),
            shape_of((rows, width), BF16),
            pltpu.HBM((3, pairs, keys, PAIR), BF16),
            shape_of((HEAD_DIM, keys), F32),
        ],
        (counts, near, far, far_core(weight), bias, far_core(cosine), far_core(sine), far_core(out_weight)),
        [
            pltpu.VMEM((3, pairs, keys, PAIR), BF16),
            pltpu.VMEM((pairs, keys, PAIR), BF16),
            pltpu.SemaphoreType.DMA((1,)),
        ],
        room=36,
    )


def middle_call(tokens, near, far, vecs):
    rows, width = tokens.shape

    def body(tok, nr, fr, vec, branch_out, fed_out):
        branch = nr[...] + fr[...].astype(F32)
        branch_out[...] = branch
        normed, _ = norm_parts(tok[...].astype(F32) + vec[2:3] * branch)
        fed_out[...] = (normed * vec[3:4] + vec[4:5]).astype(BF16)

    return call(
        body,
        (),
        [VM] * 4,
        [VM] * 2,
        [pltpu.HBM((rows, width), F32), shape_of((rows, width), BF16)],
        (tokens, near, far, vecs),
    )


def mlp_call(first, units, bits, fed, far, g, g_far, up, down, bias, before, line=None):
    rows, width = fed.shape
    tile = 256

    def body(bit, fed_in, far_in, g_in, gf_in, up_in, down_in, b_in, *rest):
        old, rest = rest[: len(before)], rest[len(before) :]
        send, keep, sums = rest[:3]
        act_out, dh_out = rest[-2:]
        step = rows // 2

        def run(down_to, up_to):
            for n in range(units // tile):
                here = slice(n * tile, (n + 1) * tile)
                there = slice(first + n * tile, first + (n + 1) * tile)
                up_w, down_w = up_in[:, there], down_in[there]
                for i in range(4):
                    x, gr = ((fed_in, g_in), (far_in, gf_in))[i // 2]
                    of, to = [slice(k * step, (k + 1) * step) for k in (i % 2, i)]
                    active, slope = gelu_parts(dot(x[of], up_w) + b_in[:, there])
                    act_out[to, here] = active.astype(BF16)
                    dh_out[to, here] = (dot(gr[of], down_w, NT) * slope).astype(BF16)
                down_to[here, :] = dot(act_out[:, here], both(g_in, gf_in), TN).astype(BF16)
                up_to[:, here] = dot(both(fed_in, far_in), dh_out[:, here], TN).astype(BF16)
                sums[:, here] = total(dh_out[:, here].astype(F32))

        pl.when(bit[0] == 0)(lambda: run(keep, send))
        pl.when(bit[0] != 0)(lambda: run(send, keep))

        if before:
            for i, place in enumerate((3, 5)):
                for k in range(2):
                    of = slice(k * rows, (k + 1) * rows)
                    low, high = old[1 - i][of], (dh_out, act_out)[i][of]
                    if i == 0:
                        value = dot(low, up_in[:, :first], NT) + dot(high, up_in[:, first:], NT)
                    else:
                        value = dot(low, down_in[:first]) + dot(high, down_in[first:])
                    rest[place + k][...] = value.astype(rest[place + k].dtype)

    both_rows = (2 * rows, units)
    out_specs = [VM] * 3
    out_shape = [pltpu.HBM((width, units), BF16)] * 2 + [shape_of((1, units), F32)]
    scratch = []
    if before:
        out_specs += [VM] * 4
        out_shape += [shape_of((rows, width), F32), shape_of((rows, width), BF16)]
        out_shape += [pltpu.HBM((rows, width), F32), pltpu.HBM((rows, width), BF16)]
        scratch = [pltpu.VMEM(both_rows, BF16)] * 2
    else:
        out_specs += [VM] * 2
        out_shape += [shape_of(both_rows, BF16)] * 2
    return call(
        body,
        (),
        [SM] + [VM] * (7 + len(before)),
        out_specs,
        out_shape,
        (bits, fed, far, g, g_far, up, down, bias, *before),
        scratch,
        line=line,
        room=16,
        cost=0,
    )


def rotary_tables(start, rows):
    quarter = HEAD_DIM // 2
    lane = lax.iota(jnp.int32, PAIR)
    frequency = 10000.0 ** (-(lane & (quarter - 1)).astype(F32) / quarter)
    sign = jnp.where((lane & quarter) == 0, -1.0, 1.0)
    order = lax.iota(jnp.int32, rows)
    places = jnp.concatenate([start + order, (rows - start) + order]).astype(F32)
    angles = places[:, None] * frequency[None, :]
    return jnp.cos(angles), jnp.sin(angles) * sign[None, :]


def input_call(normed, vecs):
    rows, width = normed.shape

    def body(n, vec, out, kept):
        value = (n[...] * vec[0:1] + vec[1:2]).astype(BF16)
        out[...] = value
        kept[...] = value

    return call(
        body,
        (),
        [VM, VM],
        [VM, VM],
        [shape_of((rows, width), BF16), pltpu.HBM((rows, width), BF16)],
        (normed, vecs),
    )


def masked(cnt, field):
    place = lax.broadcasted_iota(jnp.int32, field.shape, 0)
    return jnp.where(place < cnt[0], field.astype(F32), 0.0)


def upstream_call(counts, cotangent, vecs):
    rows, width = cotangent.shape

    def body(cnt, cot, vec, g_out, sum_out):
        g = (masked(cnt, cot[...]) * vec[5:6]).astype(BF16)
        g_out[...] = g
        sum_out[...] = total(g.astype(F32))

    return call(
        body,
        (),
        [SM, VM, VM],
        [VM, VM],
        [shape_of((rows, width), BF16), shape_of((1, width), F32)],
        (counts, cotangent, vecs),
    )


def turn_call(counts, tokens, cotangent, branch, d_near, d_far, vecs, line=None):
    rows, width = tokens.shape

    def body(cnt, tok, cot, br, dn, df, vec, dm_out, g_out, sum_out):
        normed, inverse = norm_parts(tok[...].astype(F32) + vec[2:3] * br[...])
        d_in = dn[...] + df[...].astype(F32)
        d_middle = masked(cnt, cot[...]) + norm_back(d_in * vec[3:4], normed, inverse)
        g_out[...] = (d_middle * vec[2:3]).astype(BF16)
        dm_out[...] = d_middle
        sum_out[0:1] = total(d_middle * br[...])
        sum_out[1:2] = total(d_in)
        sum_out[2:3] = total(d_in * normed)
        sum_out[3:8] = jnp.zeros((5, width), F32)

    return call(
        body,
        (),
        [SM] + [VM] * 6,
        [VM] * 3,
        [pltpu.HBM((rows, width), F32), shape_of((rows, width), BF16), shape_of((8, width), F32)],
        (counts, tokens, cotangent, branch, d_near, d_far, vecs),
        line=line,
    )


def finish_call(counts, tokens, cotangent, branch, b_near, b_far, vecs, line=None):
    rows, width = tokens.shape

    def body(cnt, tok, cot, br, bn, bf, vec, y_out, sum_out):
        middle = tok[...].astype(F32) + vec[2:3] * br[...]
        mlp_branch = bn[...] + bf[...].astype(F32) + vec[6:7]
        y_out[...] = masked(cnt, middle + vec[5:6] * mlp_branch).astype(BF16)
        sum_out[0:1] = total(masked(cnt, cot[...]) * mlp_branch)
        sum_out[1:8] = jnp.zeros((7, width), F32)

    return call(
        body,
        (),
        [SM] + [VM] * 6,
        [VM] * 2,
        [pltpu.HBM((rows, width), BF16), shape_of((8, width), F32)],
        (counts, tokens, cotangent, branch, b_near, b_far, vecs),
        line=line,
    )


def attend_back_call(bits, g, g_far, weight, qkv, e, o_t, inv, trig, cosine, sine, near, far, line=None):
    _, pairs, keys, _ = qkv.shape
    rows, width = near.shape
    half = weight.shape[0]
    quarter = HEAD_DIM // 2
    size = 3 * PAIR

    def body(bit, g_in, gf_in, inv_in, turn, w_late, ot_late, qkv_late, e_late, xn, xf, cos, sin, *rest):
        send, keep, sums = rest[:3]
        d_alls, d_in = rest[3 : 3 + pairs], rest[-1]
        d_in[...] = dot(w_late.get()[...], both(g_in, gf_in), NT).astype(BF16)
        cos_t, sin_t = turn.at[:quarter], turn.at[quarter:]

        def put(block, fill):
            at = slice((block % 2) * size, (block % 2 + 1) * size)
            pl.when(bit[0] == block // 2)(lambda: fill(keep, at))
            pl.when(bit[0] != block // 2)(lambda: fill(send, at))

        def fill_pair(j, ref, at):
            ref[:, at] = dot(both(xn.get(), xf.get()), d_alls[j][...], TN).astype(BF16)

        def fill_out(ref, at):
            grad = dot(ot_late.get()[...], both(g_in, gf_in)).astype(BF16)
            ref[:half, at] = grad[:, :half]
            ref[half:, at] = grad[:, half:]

        for j in range(pairs):
            k_t = qkv_late.get(3 * j + 1)[...].T
            v = qkv_late.get(3 * j + 2)[...]
            d_k = d_v = 0.0
            d_q = []
            for p in range(2):
                of = slice(p * rows, (p + 1) * rows)
                scaled = []
                for h in range(2):
                    hs = slice(j * PAIR + h * HEAD_DIM, j * PAIR + (h + 1) * HEAD_DIM)
                    scaled.append((d_in[hs, of].astype(F32) * inv_in[j, h, :, of]).astype(BF16))
                d_t = jnp.concatenate(scaled, axis=0)
                d = d_t.T
                q = qkv_late.get(3 * j)[of]
                halves = []
                for h in range(2):
                    hs = slice(h * HEAD_DIM, (h + 1) * HEAD_DIM)
                    ot = ot_late.get()[j * PAIR + h * HEAD_DIM : j * PAIR + (h + 1) * HEAD_DIM, of]
                    delta = total(d_t[hs].astype(F32) * ot.astype(F32))
                    d_p = dot(v, zero_other(d_t, h, 0))
                    weight = e_late.get(4 * j + 2 * p + h)[...]
                    d_s = (weight.astype(F32) * (d_p - delta)).astype(BF16)
                    d_v = d_v + dot(weight, zero_other(d, h, 1))
                    d_k = d_k + dot(d_s, zero_other(q, h, 1))
                    t = dot(k_t[hs], d_s) * HEAD_DIM ** (-0.5)
                    one, two = t[:quarter], t[quarter:]
                    halves.append((one * cos_t[:, of] + two * sin_t[:, of]).astype(BF16))
                    halves.append((two * cos_t[:, of] - one * sin_t[:, of]).astype(BF16))
                d_q.append(jnp.concatenate(halves, axis=0).T)
            u = d_k * LN2
            d_k = (u * cos.get()[...] - turn_lanes(u) * sin.get()[...]).astype(BF16)
            every = jnp.concatenate([jnp.concatenate(d_q, axis=0), d_k, d_v.astype(BF16)], axis=1)
            d_alls[j][...] = every
            xn.get(), xf.get()
            put(j, partial(fill_pair, j))
            sums[j : j + 1] = total(every.astype(F32))
        put(pairs, fill_out)

    def rank(n, i):
        if n == 7:
            return (i // 3, 1, 0)
        if n == 8:
            return (i // 4, 2, i)
        return (0, 0, n) if n < 7 else (0, 3, n)

    return call(
        body,
        (),
        [SM, VM, VM, VM, VM, Late(), Late()]
        + [Late(*[(c, j) for j in range(pairs) for c in range(3)])]
        + [Late(*[(j, h, p) for j in range(pairs) for p in range(2) for h in range(2)])]
        + [Late()] * 4,
        [VM] * (3 + pairs),
        [shape_of((width, 2 * size), BF16)] * 2
        + [shape_of((pairs, size), F32)]
        + [shape_of((keys, size), BF16)] * pairs,
        (bits, g, g_far, inv, trig, weight, o_t, qkv, e, near, far, cosine, sine),
        [pltpu.VMEM((half, keys), BF16)],
        line=line,
        room=40,
        ahead=7,
        rank=rank,
    )


def input_terms_call(parts, weight, line=None):
    keys = parts[0].shape[0]
    rows = keys // 2
    _, width, half = weight.shape

    def body(*refs):
        ins, w, near, far = refs[:-3], refs[-3], refs[-2], refs[-1]
        for i, out in enumerate((near, far)):
            acc = 0.0
            for c in range(3):
                of = slice(c * PAIR, (c + 1) * PAIR)
                d = jnp.concatenate([part[i * rows : (i + 1) * rows, of] for part in ins], axis=1)
                acc = acc + dot(d, w[c], NT)
            out[...] = acc.astype(out.dtype)

    return call(
        body,
        (),
        [VM] * (len(parts) + 1),
        [VM] * 2,
        [shape_of((rows, width), F32), shape_of((rows, width), BF16)],
        (*parts, weight),
        line=line,
        room=12,
    )


def end_call(tokens, d_middle, near, far, vecs, line=None):
    rows, width = tokens.shape

    def body(tok, dm, dn, df, vec, grad_out, sum_out):
        normed, inverse = norm_parts(tok[...].astype(F32))
        d_in = dn[...] + df[...].astype(F32)
        grad_out[...] = (dm[...] + norm_back(d_in * vec[0:1], normed, inverse)).astype(BF16)
        sum_out[0:1] = total(d_in)
        sum_out[1:2] = total(d_in * normed)
        sum_out[2:8] = jnp.zeros((6, width), F32)

    return call(
        body,
        (),
        [VM] * 5,
        [VM] * 2,
        [pltpu.HBM((rows, width), BF16), shape_of((8, width), F32)],
        (tokens, d_middle, near, far, vecs),
        line=line,
    )


def swap(value):
    return lax.ppermute(value, "tensor", [(0, 1), (1, 0)])


def bit_swap(value, bit, order_by_core):
    pairs = []
    for place in range(lax.axis_size("dp")):
        for core in range(2):
            use = bit ^ core if order_by_core else bit
            pairs.append((place * 2 + core, (place ^ (1 << use)) * 2 + core))
    return lax.ppermute(value, ("dp", "tensor"), pairs)


def pick(value, index):
    return lax.dynamic_index_in_dim(value, index, 0, keepdims=False)


def join(mine, other, index):
    return jnp.where(index == 0, jnp.stack([mine, other]), jnp.stack([other, mine]))


def bit_count():
    return lax.axis_size("dp").bit_length() - 1


def pack_call(blocks, bit, line=None):
    width, size = blocks[0].shape

    def body(b, one, two, three, four, send, keep):
        def put(low, high):
            low[:, :size], low[:, size:] = one[...], two[...]
            high[:, :size], high[:, size:] = three[...], four[...]

        pl.when(b[0] == 0)(lambda: put(keep, send))
        pl.when(b[0] != 0)(lambda: put(send, keep))

    return call(
        body,
        (),
        [SM] + [VM] * 4,
        [VM, VM],
        [shape_of((width, 2 * size), BF16)] * 2,
        (bit, *blocks),
        line=line,
    )


def shared_call(end_sums, turn_sums, out_sums, down_sums, vecs, line=None):
    width = vecs.shape[1]

    def body(ends, turn, out, down, vec, rows):
        rows[0:1] = ends[0:1]
        rows[1:2] = ends[1:2] * vec[7:8]
        rows[2:4] = turn[0:2]
        rows[4:5] = turn[2:3] * vec[8:9]
        rows[5:6] = out[0:1]
        rows[6:7] = ends[1:2] * vec[9:10]
        rows[7:8] = turn[2:3] * vec[10:11]
        rows[8:9] = down[...]
        rows[9:16] = jnp.zeros((7, width), F32)

    return call(
        body,
        (),
        [VM] * 5,
        VM,
        shape_of((16, width), F32),
        (end_sums, turn_sums, out_sums, down_sums, vecs),
        line=line,
    )


def small_call(mine, other, b_up_sums, b_qkv_sums, line=None):
    width = mine.shape[1]
    half = width // 2

    def body(one, two, up_0, up_1, qkv_0, qkv_1, qkv_2, rows):
        rows[...] = jnp.concatenate(
            [
                (one[...] + two[...])[:9],
                up_0[...],
                up_1[...],
                jnp.concatenate([qkv_0[...], qkv_1[...]], axis=1),
                jnp.concatenate([qkv_2[...], jnp.zeros((1, half), F32)], axis=1),
                jnp.zeros((3, width), F32),
            ],
            axis=0,
        ).astype(BF16)

    return call(
        body,
        (),
        [VM] * 7,
        VM,
        shape_of((16, width), BF16),
        (mine, other, *b_up_sums, *b_qkv_sums),
        line=line,
    )


def append_call(mine, other, line=None):
    rows, width = mine.shape

    def body(one, two, out):
        out[:rows] = one[...]
        out[rows:] = two[...]

    return call(
        body, (), [VM, VM], VM, shape_of((2 * rows, width), BF16), (mine, other), line=line
    )


def split_add(mine, other, bit, line=None):
    rows, width = mine.shape

    def body(b, one, two, send, keep):
        field = (one[...].astype(F32) + two[...].astype(F32)).astype(BF16)
        low, high = field[: rows // 2], field[rows // 2 :]

        @pl.when(b[0] == 0)
        def _():
            keep[...] = low
            send[...] = high

        @pl.when(b[0] != 0)
        def _():
            send[...] = low
            keep[...] = high

    return call(
        body,
        (),
        [SM, VM, VM],
        [VM, VM],
        [shape_of((rows // 2, width), BF16)] * 2,
        (bit, mine, other),
        line=line,
    )


def plain_add(mine, other, line=None):
    def body(one, two, out):
        out[...] = (one[...].astype(F32) + two[...].astype(F32)).astype(BF16)

    return call(
        body, (), [VM, VM], VM, shape_of(mine.shape, BF16), (mine, other), line=line
    )


def stack_halves(mine, other, bit, line=None):
    rows, width = mine.shape

    def body(b, one, two, out):
        out[pl.ds(pl.multiple_of(b[0] * rows, rows), rows)] = one[...]
        out[pl.ds(pl.multiple_of((1 - b[0]) * rows, rows), rows)] = two[...]

    return call(
        body,
        (),
        [SM, VM, VM],
        VM,
        shape_of((2 * rows, width), BF16),
        (bit, mine, other),
        line=line,
    )


def unpack_call(mine, other, bit, before, units, at, line=None):
    width = mine.shape[0]
    size = mine.shape[1]

    def body(b, one, two, *rest):
        down_out, up_out = rest[-2:]

        @pl.when(b[0] == 0)
        def _():
            down_out[...] = one[...].astype(F32)
            up_out[...] = two[...].astype(F32)

        @pl.when(b[0] != 0)
        def _():
            down_out[...] = two[...].astype(F32)
            up_out[...] = one[...].astype(F32)

    extra = [pl.BlockSpec(memory_space=pl.ANY)] * len(before)
    return call(
        body,
        (1,),
        [SM, whole(mine.shape), whole(mine.shape)] + extra,
        [
            pl.BlockSpec((size, width), lambda i: (at, 0)),
            pl.BlockSpec((width, size), lambda i: (0, at)),
        ],
        [pltpu.HBM((units, width), F32), pltpu.HBM((width, units), F32)],
        (bit, mine, other) + tuple(far_core(x) for x in before),
        line=line,
        aliases={3: 0, 4: 1} if before else None,
        room=16,
    )


def unpack_last_call(mine, other, bit, line=None):
    width, size = mine.shape
    half = size // 2

    def body(b, one, two, qkv_out, out_out):
        def put(low, high):
            for j, block in enumerate((low[:, :half], low[:, half:], high[:, :half])):
                for c in range(3):
                    qkv_out[c, :, j * PAIR : (j + 1) * PAIR] = block[:, c * PAIR : (c + 1) * PAIR].astype(F32)
            out_out[:, :half] = high[:half, half:].astype(F32)
            out_out[:, half:] = high[half:, half:].astype(F32)

        pl.when(b[0] == 0)(lambda: put(one, two))
        pl.when(b[0] != 0)(lambda: put(two, one))

    return call(
        body,
        (),
        [SM, VM, VM],
        [VM, VM],
        [pltpu.HBM((3, width, half), F32), pltpu.HBM((half, width), F32)],
        (bit, mine, other),
        line=line,
    )


def reduce_steps(send, keep, bits, halve, line):
    first, second, third = bits
    other = bit_swap(send, 0, True)
    yield other
    send, keep = split_add(keep, other, second, line)
    other = bit_swap(send, 1, True)
    yield other
    if halve:
        send, keep = split_add(keep, other, third, line)
        other = bit_swap(send, 2, False)
        yield other
        mine = plain_add(keep, other, line)
    else:
        mine = plain_add(keep, other, line)
        other = bit_swap(mine, 2, False)
        yield other
        mine = plain_add(mine, other, line)
    for bit in range(3, bit_count()):
        other = bit_swap(mine, bit, False)
        yield other
        mine = plain_add(mine, other, line)
    if halve:
        other = bit_swap(mine, 2, False)
        yield other
        mine = stack_halves(mine, other, third, line)
    other = bit_swap(mine, 1, True)
    yield other
    mine = stack_halves(mine, other, second, line)
    yield mine, bit_swap(mine, 0, True)


class Gather:
    def __init__(self, value, line):
        self.line = line
        self.value = value
        self.bit = 0
        self.other = bit_swap(value, 0, False)

    def go(self):
        if self.bit < bit_count():
            self.value = append_call(self.value, self.other, self.line)
            self.bit += 1
            if self.bit < bit_count():
                self.other = bit_swap(self.value, self.bit, False)

    def all(self):
        while self.bit < bit_count():
            self.go()
        return self.value


def tree_sum(value):
    while value.shape[0] > 1:
        value = value.reshape((-1, 2) + value.shape[1:])
        value = value[:, 0] + value[:, 1]
    return value[0]


class Line:
    def __init__(self):
        self.turn = jnp.zeros((8, 128), F32)

    def go(self):
        raise ValueError("unknown step")


class Group:
    def __init__(self, name, send, keep, bits, line, halve=True):
        self.name = name
        self.steps = reduce_steps(send, keep, bits, halve, line)
        with jax.named_scope(name):
            self.waiting = next(self.steps)

    def go(self):
        if not isinstance(self.waiting, tuple):
            self.waiting = next(self.steps)

    def halves(self):
        while not isinstance(self.waiting, tuple):
            self.go()
        return self.waiting


def shards(
    tokens,
    temb,
    lengths,
    w_mod,
    b_mod,
    gain_attn,
    query_key_value_weight,
    b_qkv,
    attention_output_weight,
    gain_mlp,
    up_weight,
    b_up,
    down_weight,
    b_down,
    cotangent,
):
    tokens, cotangent, length = tokens[0], cotangent[0], lengths[0]
    rows, width = tokens.shape
    core = lax.axis_index("tensor")
    place = lax.axis_index("dp")
    bits = [
        jnp.reshape((place >> b) & 1, (1,)).astype(jnp.int32) for b in (core, 1 - core, jnp.int32(2))
    ]
    half = width // 2
    start = core * rows
    counts = jnp.clip(jnp.stack([length - start, length - (rows - start)]), 0, rows)

    qkv_weight = jnp.swapaxes(query_key_value_weight, 0, 1)
    embed_part = lax.all_to_all(temb, "dp", split_axis=1, concat_axis=0, tiled=True)
    later, later_start, b_qkv, b_up, b_mod, b_down, gain_attn, gain_mlp, embed_part = lax.optimization_barrier(
        (tokens, start, b_qkv, b_up, b_mod, b_down, gain_attn, gain_mlp, embed_part)
    )
    qkv_bias = b_qkv.reshape(3, 1, half).astype(F32)
    up_bias = b_up.reshape(1, -1).astype(F32)
    normed_attn, _ = norm_parts(later.astype(F32))
    cosine, sine = rotary_tables(later_start, rows)
    mod_terms = jnp.dot(embed_part, w_mod, preferred_element_type=F32)
    mod_terms = lax.all_to_all(mod_terms, "dp", split_axis=0, concat_axis=0, tiled=True)
    mod_terms, cosine, sine, normed_attn, qkv_bias, up_bias = lax.optimization_barrier(
        (mod_terms, cosine, sine, normed_attn, qkv_bias, up_bias)
    )
    modulation = jnp.sum(mod_terms, axis=0) + b_mod.astype(F32)
    shift_attn, scale_attn, gate_attn, shift_mlp, scale_mlp, gate_mlp = modulation.reshape(6, width)
    gain_attn = gain_attn.astype(F32)
    gain_mlp = gain_mlp.astype(F32)
    vecs = jnp.stack(
        [
            gain_attn * (1.0 + scale_attn),
            shift_attn,
            gate_attn,
            gain_mlp * (1.0 + scale_mlp),
            shift_mlp,
            gate_mlp,
            b_down.astype(F32),
            gain_attn,
            gain_mlp,
            1.0 + scale_attn,
            1.0 + scale_mlp,
        ]
    )

    attn_in, x_near = input_call(normed_attn, vecs)
    attn_in_far = swap(attn_in)
    g_mlp, down_sums = upstream_call(counts, cotangent, vecs)
    g_mlp_far = swap(g_mlp)
    e, o_t, inv, branch_near, branch_far, qkv, trig = attend_call(
        counts, attn_in, attn_in_far, qkv_weight, qkv_bias, cosine, sine, attention_output_weight
    )
    attn_branch, fed = middle_call(tokens, branch_near, swap(branch_far), vecs)
    fed_far = swap(fed)
    units = up_weight.shape[1]
    size = units // 2
    line = Line()
    b_up_sums, groups, made = [], {}, {}
    before = ()
    for part, name in enumerate(("mlp_first", "mlp_second")):
        send, keep, b_up_sum, *before = mlp_call(
            part * size, size, bits[0], fed, fed_far, g_mlp, g_mlp_far, up_weight, down_weight, up_bias, before, line
        )
        groups[name] = Group(name, send, keep, bits, line)
        b_up_sums.append(b_up_sum)
    made["d_near"], d_far, made["b_near"], b_far = before
    made["d_far"] = swap(d_far)
    made["b_far"] = swap(b_far)

    def turn():
        made["d_middle"], g_attn, made["turn_sums"] = turn_call(
            counts, tokens, cotangent, attn_branch, made["d_near"], made["d_far"], vecs, line
        )
        made["g"] = (g_attn, swap(g_attn))
        made["x_far"] = swap(lax.optimization_barrier((x_near, g_attn))[0])

    def back():
        send, keep, sums, *made["d_alls"] = attend_back_call(
            bits[0], *made["g"], attention_output_weight, qkv, e, o_t, inv, trig, cosine, sine, x_near, made["x_far"], line
        )
        made["b_qkv"] = [sums[n : n + 1] for n in range(sums.shape[0])]
        groups["projections"] = Group("projections", send, keep, bits, line)

    def d_attn_in():
        made["a_near"], a_far = input_terms_call(made["d_alls"], qkv_weight, line)
        made["a_far"] = swap(a_far)

    def finish():
        made["output"], made["out_sums"] = finish_call(
            counts, tokens, cotangent, attn_branch, made["b_near"], made["b_far"], vecs, line
        )

    def end():
        made["grad_tokens"], made["end_sums"] = end_call(
            tokens, made["d_middle"], made["a_near"], made["a_far"], vecs, line
        )

    def share():
        shared = shared_call(made["end_sums"], made["turn_sums"], made["out_sums"], down_sums, vecs, line)
        made["shared"] = (shared, swap(shared))

    def small():
        rows = small_call(*made["shared"], b_up_sums, made["b_qkv"], line)
        groups["small"] = Gather(rows, line)

    def unpack(at, name):
        made["totals"] = unpack_call(*groups[name].halves(), bits[0], made.get("totals", ()), units, at, line)

    acts = [turn, back, d_attn_in, finish, end, share, small]
    acts = {act.__name__: act for act in acts}
    gather = acts.pop("small")
    acts["begin"] = gather
    acts["unpack_first"] = lambda: unpack(0, "mlp_first")
    acts["unpack_second"] = lambda: unpack(1, "mlp_second")
    for word in ORDER:
        with jax.named_scope(word):
            acts.get(word, groups.get(word, line).go)()
    groups["projections"].halves()
    every = groups["small"].all().reshape(-1, 16, width)
    grad_mod_all = every[:, :6].reshape(-1, 6 * width)
    embed_order = lax.iota(jnp.int32, every.shape[0]) ^ place
    embed_here = jnp.take(embed_part, embed_order, axis=0)
    grad_w_mod = dot(embed_here, grad_mod_all, TN)
    embed_terms = jnp.take(dot(grad_mod_all, w_mod, NT), embed_order, axis=0)
    grad_temb = lax.all_to_all(embed_terms, "dp", split_axis=0, concat_axis=1, tiled=True)
    sums = tree_sum(every.astype(F32))
    output, grad_tokens, totals = made["output"], made["grad_tokens"], made["totals"]
    down_total, up_total = totals
    qkv_total, out_total = unpack_last_call(*groups["projections"].halves(), bits[0], line)
    b_up_total = sums[9:11].reshape(-1)
    b_qkv_total = sums[11:13].reshape(-1)[: 9 * PAIR].reshape(3, 3, PAIR)
    return (
        output[None],
        grad_tokens[None],
        grad_temb,
        grad_w_mod,
        sums[:6].reshape(-1),
        sums[6],
        jnp.swapaxes(qkv_total, 0, 1),
        jnp.swapaxes(b_qkv_total, 0, 1).reshape(3, half),
        out_total,
        sums[7],
        up_total,
        b_up_total,
        down_total,
        sums[8],
    )


def solution(mesh):
    return jax.shard_map(
        shards,
        mesh=mesh,
        in_specs=(
            P("dp", "tensor", None),
            P("dp", None),
            P("dp"),
            P("dp", None),
            P(),
            P(),
            P(None, None, "tensor"),
            P(None, "tensor"),
            P("tensor", None),
            P(),
            P(None, "tensor"),
            P("tensor"),
            P("tensor", None),
            P(),
            P("dp", "tensor", None),
        ),
        out_specs=(
            P("dp", "tensor", None),
            P("dp", "tensor", None),
            P("dp", None),
            P("dp", None),
            P(),
            P(),
            P(None, None, "tensor"),
            P(None, "tensor"),
            P("tensor", None),
            P(),
            P(None, "tensor"),
            P("tensor"),
            P("tensor", None),
            P(),
        ),
        check_vma=False,
    )
```

```python
from functools import partial
from math import log, pi, sqrt

import jax
import jax.numpy as jnp
from jax import lax
from jax.experimental import pallas as pl
from jax.experimental.pallas import tpu as pltpu
from jax.sharding import PartitionSpec as P

HEAD_DIM = 64
PAIR = 2 * HEAD_DIM
F32 = jnp.float32
BF16 = jnp.bfloat16
NN = ((1,), (0,))
NT = ((1,), (1,))
TN = ((0,), (0,))
SAFE = 90.0
LONG = 10**9
ORDER = (
    "mlp_first", "turn", "back", "mlp_second", "mlp_first", "d_attn_in", "mlp_second", "mlp_first",
    "finish", "end", "share", "mlp_second", "projections", "mlp_first", "projections", "begin",
    "mlp_first", "mlp_second", "projections", "small", "mlp_first", "projections", "small",
    "mlp_second", "unpack_first", "projections", "mlp_second", "small", "projections", "small",
    "unpack_second", "mod_back",
)
LN2 = log(2.0)
MIB = 1024 * 1024
VM = pl.BlockSpec(memory_space=pltpu.VMEM)
SM = pl.BlockSpec(memory_space=pltpu.SMEM)
HB = pl.BlockSpec(memory_space=pltpu.HBM)


def dot(left, right, dims=NN):
    return lax.dot_general(left, right, (dims, ((), ())), preferred_element_type=F32)


class Late:
    def __init__(self, *parts):
        self.parts = parts or ((),)


class Queue:
    def __init__(self, copies, ahead):
        self.copies = copies
        self.started = 0
        self.here = set()
        self.start(ahead)

    def start(self, count):
        for copy in self.copies[self.started : self.started + count]:
            copy.start()
        self.started += count

    def need(self, n):
        if n not in self.here:
            self.start(max(0, n + 1 - self.started))
            self.here.add(n)
            self.copies[n].wait()
            self.start(1)


class LateRef:
    def __init__(self, queue, places, refs):
        self.queue = queue
        self.places = places
        self.refs = refs

    def get(self, n=0):
        self.queue.need(self.places[n])
        return self.refs[n]


def call(body, grid, in_specs, out_specs, out_shape, args, scratch=(), line=None, room=12, aliases=None, ahead=3, rank=None, cost=None):
    count = len(in_specs)
    single = not isinstance(out_shape, list)
    out_specs = [out_specs] if single else list(out_specs)
    out_shape = [out_shape] if single else list(out_shape)
    outs = len(out_shape)
    late = [n for n, spec in enumerate(in_specs) if isinstance(spec, Late)]
    pieces = [(n, part) for n in late for part in in_specs[n].parts]
    if rank is not None:
        pieces.sort(key=lambda piece: rank(piece[0], in_specs[piece[0]].parts.index(piece[1])))
    buffers = [
        pltpu.VMEM(jax.eval_shape(lambda x, part=part: x[part], args[n]).shape, args[n].dtype)
        for n, part in pieces
    ]
    args = [far_core(arg) if n in late else arg for n, arg in enumerate(args)]
    in_specs = [HB if n in late else spec for n, spec in enumerate(in_specs)]
    if pieces:
        buffers.append(pltpu.SemaphoreType.DMA((len(pieces),)))
    extra = 0
    if line is not None:
        extra = 1
        cost = LONG if cost is None else cost
        in_specs.append(pl.BlockSpec(memory_space=pl.ANY))
        args.append(line.turn)
        out_specs.append(VM)
        out_shape.append(shape_of((8, 128), F32))

    def wrapped(*refs):
        ins = list(refs[:count])
        rest = list(refs[count + extra : count + extra + outs])
        if extra:
            refs[count + extra + outs][...] = jnp.zeros((8, 128), F32)
        rest += refs[count + 2 * extra + outs :]
        if pieces:
            rest, held, sems = rest[: -len(buffers)], rest[-len(buffers) : -1], rest[-1]
            copies = []
            for i, (n, part) in enumerate(pieces):
                source = ins[n].at[part] if part else ins[n]
                copies.append(pltpu.make_async_copy(source, held[i], sems.at[i]))
            queue = Queue(copies, ahead)
            for n in late:
                mine = [i for i, (m, _) in enumerate(pieces) if m == n]
                ins[n] = LateRef(queue, mine, [held[i] for i in mine])
        body(*ins, *rest)
        if pieces:
            for i in range(len(pieces)):
                queue.need(i)

    result = pl.pallas_call(
        wrapped,
        grid=grid,
        in_specs=in_specs,
        out_specs=out_specs,
        out_shape=out_shape,
        scratch_shapes=list(scratch) + buffers,
        input_output_aliases=aliases or {},
        compiler_params=pltpu.CompilerParams(
            vmem_limit_bytes=room * MIB, dimension_semantics=("arbitrary",) * len(grid)
        ),
        cost_estimate=pl.CostEstimate(flops=cost or 0, bytes_accessed=0, transcendentals=0),
    )(*args)
    if extra:
        line.turn = result[-1]
        result = result[:-1]
    return result[0] if single else result


def whole(shape):
    return pl.BlockSpec(shape, lambda *_: (0,) * len(shape))


def shape_of(shape, kind):
    return pltpu.VMEM(shape, kind)


def far_core(value):
    return pltpu.with_memory_space_constraint(value, pltpu.HBM)


def norm_parts(field):
    centred = field - jnp.mean(field, axis=-1, keepdims=True)
    inverse = lax.rsqrt(jnp.mean(centred * centred, axis=-1, keepdims=True) + 1e-05)
    return (centred * inverse, inverse)


def norm_back(upstream, normed, inverse):
    return inverse * (
        upstream
        - jnp.mean(upstream, axis=-1, keepdims=True)
        - normed * jnp.mean(upstream * normed, axis=-1, keepdims=True)
    )


def gelu_parts(hidden):
    scale = sqrt(2.0 / pi)
    square = hidden * hidden
    bent = jnp.tanh(hidden * (scale + (scale * 0.044715) * square))
    upper = 0.5 + 0.5 * bent
    slope = upper + (hidden * (0.5 - 0.5 * bent * bent)) * (scale + (3 * 0.044715 * scale) * square)
    return (hidden * upper, slope)


def turn_lanes(field):
    lane = lax.broadcasted_iota(jnp.int32, field.shape, 1)
    up = pltpu.roll(field, PAIR - HEAD_DIM // 2, 1)
    down = pltpu.roll(field, HEAD_DIM // 2, 1)
    return jnp.where((lane & (HEAD_DIM - 1)) < HEAD_DIM // 2, up, down)


def zero_other(field, h, axis):
    place = lax.broadcasted_iota(jnp.int32, field.shape, axis)
    return jnp.where((place >= HEAD_DIM) == (h == 1), field, jnp.zeros_like(field))


def total(field):
    return jnp.sum(field, axis=0, keepdims=True)


def both(near, far):
    return jnp.concatenate([near[...], far[...]], axis=0)


def attend_call(counts, near, far, weight, bias, cosine, sine, out_weight):
    rows, width = near.shape
    keys = 2 * rows
    half = weight.shape[2]
    pairs = half // PAIR
    quarter = HEAD_DIM // 2

    def body(
        cnt, xn, xf, w, b, cos, sin, w_out, e_out, ot_out, inv_out, near_out, far_out, qkv_out, trig, qkv, o_all, sem
    ):
        j = pl.program_id(0)
        store = pltpu.make_async_copy(qkv, qkv_out, sem.at[0])

        @pl.when(j == 0)
        def _():
            for c in range(3):
                for i, x in enumerate((xn, xf)):
                    here = slice(i * rows, (i + 1) * rows)
                    y = dot(x[...], w[c]) + b[c]
                    for n in range(pairs):
                        u = y[:, n * PAIR : (n + 1) * PAIR]
                        if c < 2:
                            u = u * cos[here] + turn_lanes(u) * sin[here]
                        if c == 0:
                            u = u * (HEAD_DIM ** (-0.5) / LN2)
                        qkv[c, n, here] = u.astype(BF16)
            trig[:quarter] = cos[...].T[:quarter]
            trig[quarter:] = sin[...].T[quarter : 2 * quarter]
            store.start()

        q_in = qkv.at[0, j]
        k = qkv[1, j]
        v_t = qkv[2, j].T
        near_count, far_count = cnt[0], cnt[1]

        def run(masked, plain):
            for p in range(2):
                of = slice(p * rows, (p + 1) * rows)
                q_t = q_in[of].T
                for h in range(2):
                    hs = slice(h * HEAD_DIM, (h + 1) * HEAD_DIM)
                    s = dot(k, zero_other(q_t, h, 0))
                    if masked:
                        place = lax.broadcasted_iota(jnp.int32, (keys, rows), 0)
                        limit = jnp.where(place < rows, near_count, rows + far_count)
                        s = jnp.where(place < limit, s, -1e30)
                    if not plain:
                        s = s - jnp.max(s, axis=0, keepdims=True)
                    e = jnp.exp2(s)
                    inv = 1.0 / total(e)
                    e = e.astype(BF16)
                    e_out[0, h, p] = e
                    inv_out[0, h, :, of] = inv
                    ot_out[hs, of] = (dot(v_t[hs], e) * inv).astype(BF16)

        def norms(field):
            square = field.astype(F32) * field.astype(F32)
            return [
                jnp.max(jnp.sum(zero_other(square, h, 1), axis=1, keepdims=True)) for h in range(2)
            ]

        bound = 0.0
        for one, two in zip(norms(q_in[...]), norms(k)):
            bound = jnp.maximum(bound, one * two)
        plain = bound < SAFE * SAFE
        everything = near_count + far_count >= keys
        pl.when(plain & everything)(lambda: run(False, True))
        pl.when(plain & jnp.logical_not(everything))(lambda: run(True, True))
        pl.when(jnp.logical_not(plain))(lambda: run(True, False))
        o_all[j] = ot_out[...].T

        @pl.when(j == pairs - 1)
        def _():
            o = jnp.concatenate([o_all[i] for i in range(pairs)], axis=1)
            near_out[...] = dot(o[:rows], w_out[...])
            far_out[...] = dot(o[rows:], w_out[...]).astype(BF16)
            store.wait()

    return call(
        body,
        (pairs,),
        [
            SM,
            whole((rows, width)),
            whole((rows, width)),
            whole((3, width, half)),
            whole((3, 1, half)),
            whole((keys, PAIR)),
            whole((keys, PAIR)),
            whole((half, width)),
        ],
        [
            pl.BlockSpec((1, 2, 2, keys, rows), lambda j: (j, 0, 0, 0, 0)),
            pl.BlockSpec((PAIR, keys), lambda j: (j, 0)),
            pl.BlockSpec((1, 2, 1, keys), lambda j: (j, 0, 0, 0)),
            whole((rows, width)),
            whole((rows, width)),
            HB,
            whole((HEAD_DIM, keys)),
        ],
        [
            pltpu.HBM((pairs, 2, 2, keys, rows), BF16),
            pltpu.HBM((half, keys), BF16),
            shape_of((pairs, 2, 1, keys), F32),
            shape_of((rows, width), F32),
            shape_of((rows, width), BF16),
            pltpu.HBM((3, pairs, keys, PAIR), BF16),
            shape_of((HEAD_DIM, keys), F32),
        ],
        (counts, near, far, far_core(weight), bias, far_core(cosine), far_core(sine), far_core(out_weight)),
        [
            pltpu.VMEM((3, pairs, keys, PAIR), BF16),
            pltpu.VMEM((pairs, keys, PAIR), BF16),
            pltpu.SemaphoreType.DMA((1,)),
        ],
        room=36,
    )


def middle_call(tokens, near, far, vecs):
    rows, width = tokens.shape

    def body(tok, nr, fr, vec, branch_out, fed_out):
        branch = nr[...] + fr[...].astype(F32)
        branch_out[...] = branch
        normed, _ = norm_parts(tok[...].astype(F32) + vec[2:3] * branch)
        fed_out[...] = (normed * vec[3:4] + vec[4:5]).astype(BF16)

    return call(
        body,
        (),
        [VM] * 4,
        [VM] * 2,
        [pltpu.HBM((rows, width), F32), shape_of((rows, width), BF16)],
        (tokens, near, far, vecs),
    )


def mlp_call(first, units, bits, fed, far, g, g_far, up, down, bias, before, line=None):
    rows, width = fed.shape
    tile = 256

    def body(bit, fed_in, far_in, g_in, gf_in, up_in, down_in, b_in, *rest):
        old, rest = rest[: len(before)], rest[len(before) :]
        send, keep, sums = rest[:3]
        act_out, dh_out = rest[-2:]
        step = rows // 2

        def run(down_to, up_to):
            for n in range(units // tile):
                here = slice(n * tile, (n + 1) * tile)
                there = slice(first + n * tile, first + (n + 1) * tile)
                up_w, down_w = up_in[:, there], down_in[there]
                for i in range(4):
                    x, gr = ((fed_in, g_in), (far_in, gf_in))[i // 2]
                    of, to = [slice(k * step, (k + 1) * step) for k in (i % 2, i)]
                    active, slope = gelu_parts(dot(x[of], up_w) + b_in[:, there])
                    act_out[to, here] = active.astype(BF16)
                    dh_out[to, here] = (dot(gr[of], down_w, NT) * slope).astype(BF16)
                down_to[here, :] = dot(act_out[:, here], both(g_in, gf_in), TN).astype(BF16)
                up_to[:, here] = dot(both(fed_in, far_in), dh_out[:, here], TN).astype(BF16)
                sums[:, here] = total(dh_out[:, here].astype(F32))

        pl.when(bit[0] == 0)(lambda: run(keep, send))
        pl.when(bit[0] != 0)(lambda: run(send, keep))

        if before:
            for i, place in enumerate((3, 5)):
                for k in range(2):
                    of = slice(k * rows, (k + 1) * rows)
                    low, high = old[1 - i][of], (dh_out, act_out)[i][of]
                    if i == 0:
                        value = dot(low, up_in[:, :first], NT) + dot(high, up_in[:, first:], NT)
                    else:
                        value = dot(low, down_in[:first]) + dot(high, down_in[first:])
                    rest[place + k][...] = value.astype(rest[place + k].dtype)

    both_rows = (2 * rows, units)
    out_specs = [VM] * 3
    out_shape = [pltpu.HBM((width, units), BF16)] * 2 + [shape_of((1, units), F32)]
    scratch = []
    if before:
        out_specs += [VM] * 4
        out_shape += [shape_of((rows, width), F32), shape_of((rows, width), BF16)]
        out_shape += [pltpu.HBM((rows, width), F32), pltpu.HBM((rows, width), BF16)]
        scratch = [pltpu.VMEM(both_rows, BF16)] * 2
    else:
        out_specs += [VM] * 2
        out_shape += [shape_of(both_rows, BF16)] * 2
    return call(
        body,
        (),
        [SM] + [VM] * (7 + len(before)),
        out_specs,
        out_shape,
        (bits, fed, far, g, g_far, up, down, bias, *before),
        scratch,
        line=line,
        room=16,
        cost=0,
    )


def rotary_tables(start, rows):
    quarter = HEAD_DIM // 2
    lane = lax.iota(jnp.int32, PAIR)
    frequency = 10000.0 ** (-(lane & (quarter - 1)).astype(F32) / quarter)
    sign = jnp.where((lane & quarter) == 0, -1.0, 1.0)
    order = lax.iota(jnp.int32, rows)
    places = jnp.concatenate([start + order, (rows - start) + order]).astype(F32)
    angles = places[:, None] * frequency[None, :]
    return jnp.cos(angles), jnp.sin(angles) * sign[None, :]


def input_call(normed, vecs):
    rows, width = normed.shape

    def body(n, vec, out, kept):
        value = (n[...] * vec[0:1] + vec[1:2]).astype(BF16)
        out[...] = value
        kept[...] = value

    return call(
        body,
        (),
        [VM, VM],
        [VM, VM],
        [shape_of((rows, width), BF16), pltpu.HBM((rows, width), BF16)],
        (normed, vecs),
    )


def carry_call(after, *weights):
    count = len(weights)

    def body(*refs):
        ins, outs, sems = refs[1 : 1 + count], refs[1 + count : -1], refs[-1]
        copies = [pltpu.make_async_copy(a, b, sems.at[n]) for n, (a, b) in enumerate(zip(ins, outs))]
        for copy in copies:
            copy.start()
        for copy in copies:
            copy.wait()

    return call(
        body,
        (),
        [pl.BlockSpec(memory_space=pl.ANY)] + [HB] * count,
        [pl.BlockSpec(memory_space=pl.ANY)] * count,
        [shape_of(weight.shape, BF16) for weight in weights],
        (after, *[far_core(weight) for weight in weights]),
        [pltpu.SemaphoreType.DMA((count,))],
        room=1,
    )


def masked(cnt, field):
    place = lax.broadcasted_iota(jnp.int32, field.shape, 0)
    return jnp.where(place < cnt[0], field.astype(F32), 0.0)


def upstream_call(counts, cotangent, vecs):
    rows, width = cotangent.shape

    def body(cnt, cot, vec, g_out, sum_out):
        g = (masked(cnt, cot[...]) * vec[5:6]).astype(BF16)
        g_out[...] = g
        sum_out[...] = total(g.astype(F32))

    return call(
        body,
        (),
        [SM, VM, VM],
        [VM, VM],
        [shape_of((rows, width), BF16), shape_of((1, width), F32)],
        (counts, cotangent, vecs),
    )


def turn_call(counts, tokens, cotangent, branch, d_near, d_far, vecs, line=None):
    rows, width = tokens.shape

    def body(cnt, tok, cot, br, dn, df, vec, dm_out, g_out, sum_out):
        normed, inverse = norm_parts(tok[...].astype(F32) + vec[2:3] * br[...])
        d_in = dn[...] + df[...].astype(F32)
        d_middle = masked(cnt, cot[...]) + norm_back(d_in * vec[3:4], normed, inverse)
        g_out[...] = (d_middle * vec[2:3]).astype(BF16)
        dm_out[...] = d_middle
        sum_out[0:1] = total(d_middle * br[...])
        sum_out[1:2] = total(d_in)
        sum_out[2:3] = total(d_in * normed)
        sum_out[3:8] = jnp.zeros((5, width), F32)

    return call(
        body,
        (),
        [SM] + [VM] * 6,
        [VM] * 3,
        [pltpu.HBM((rows, width), F32), shape_of((rows, width), BF16), shape_of((8, width), F32)],
        (counts, tokens, cotangent, branch, d_near, d_far, vecs),
        line=line,
    )


def finish_call(counts, tokens, cotangent, branch, b_near, b_far, vecs, line=None):
    rows, width = tokens.shape

    def body(cnt, tok, cot, br, bn, bf, vec, y_out, sum_out):
        middle = tok[...].astype(F32) + vec[2:3] * br[...]
        mlp_branch = bn[...] + bf[...].astype(F32) + vec[6:7]
        y_out[...] = masked(cnt, middle + vec[5:6] * mlp_branch).astype(BF16)
        sum_out[0:1] = total(masked(cnt, cot[...]) * mlp_branch)
        sum_out[1:8] = jnp.zeros((7, width), F32)

    return call(
        body,
        (),
        [SM] + [VM] * 6,
        [VM] * 2,
        [pltpu.HBM((rows, width), BF16), shape_of((8, width), F32)],
        (counts, tokens, cotangent, branch, b_near, b_far, vecs),
        line=line,
    )


def attend_back_call(bits, g, g_far, weight, qkv, e, o_t, inv, trig, cosine, sine, near, far, line=None):
    _, pairs, keys, _ = qkv.shape
    rows, width = near.shape
    half = weight.shape[0]
    quarter = HEAD_DIM // 2
    size = 3 * PAIR

    def body(bit, g_in, gf_in, inv_in, turn, w_late, ot_late, qkv_late, e_late, xn, xf, cos, sin, *rest):
        send, keep, sums = rest[:3]
        d_alls, d_in = rest[3 : 3 + pairs], rest[-1]
        d_in[...] = dot(w_late.get()[...], both(g_in, gf_in), NT).astype(BF16)
        cos_t, sin_t = turn.at[:quarter], turn.at[quarter:]

        def put(block, fill):
            at = slice((block % 2) * size, (block % 2 + 1) * size)
            pl.when(bit[0] == block // 2)(lambda: fill(keep, at))
            pl.when(bit[0] != block // 2)(lambda: fill(send, at))

        def fill_pair(j, ref, at):
            ref[:, at] = dot(both(xn.get(), xf.get()), d_alls[j][...], TN).astype(BF16)

        def fill_out(ref, at):
            grad = dot(ot_late.get()[...], both(g_in, gf_in)).astype(BF16)
            ref[:half, at] = grad[:, :half]
            ref[half:, at] = grad[:, half:]

        for j in range(pairs):
            k_t = qkv_late.get(3 * j + 1)[...].T
            v = qkv_late.get(3 * j + 2)[...]
            d_k = d_v = 0.0
            d_q = []
            for p in range(2):
                of = slice(p * rows, (p + 1) * rows)
                scaled = []
                for h in range(2):
                    hs = slice(j * PAIR + h * HEAD_DIM, j * PAIR + (h + 1) * HEAD_DIM)
                    scaled.append((d_in[hs, of].astype(F32) * inv_in[j, h, :, of]).astype(BF16))
                d_t = jnp.concatenate(scaled, axis=0)
                d = d_t.T
                q = qkv_late.get(3 * j)[of]
                halves = []
                for h in range(2):
                    hs = slice(h * HEAD_DIM, (h + 1) * HEAD_DIM)
                    ot = ot_late.get()[j * PAIR + h * HEAD_DIM : j * PAIR + (h + 1) * HEAD_DIM, of]
                    delta = total(d_t[hs].astype(F32) * ot.astype(F32))
                    d_p = dot(v, zero_other(d_t, h, 0))
                    weight = e_late.get(4 * j + 2 * p + h)[...]
                    d_s = (weight.astype(F32) * (d_p - delta)).astype(BF16)
                    d_v = d_v + dot(weight, zero_other(d, h, 1))
                    d_k = d_k + dot(d_s, zero_other(q, h, 1))
                    t = dot(k_t[hs], d_s) * HEAD_DIM ** (-0.5)
                    one, two = t[:quarter], t[quarter:]
                    halves.append((one * cos_t[:, of] + two * sin_t[:, of]).astype(BF16))
                    halves.append((two * cos_t[:, of] - one * sin_t[:, of]).astype(BF16))
                d_q.append(jnp.concatenate(halves, axis=0).T)
            u = d_k * LN2
            d_k = (u * cos.get()[...] - turn_lanes(u) * sin.get()[...]).astype(BF16)
            every = jnp.concatenate([jnp.concatenate(d_q, axis=0), d_k, d_v.astype(BF16)], axis=1)
            d_alls[j][...] = every
            xn.get(), xf.get()
            put(j, partial(fill_pair, j))
            sums[j : j + 1] = total(every.astype(F32))
        put(pairs, fill_out)

    def rank(n, i):
        if n == 7:
            return (i // 3, 1, 0)
        if n == 8:
            return (i // 4, 2, i)
        return (0, 0, n) if n < 7 else (0, 3, n)

    return call(
        body,
        (),
        [SM, VM, VM, VM, VM, Late(), Late()]
        + [Late(*[(c, j) for j in range(pairs) for c in range(3)])]
        + [Late(*[(j, h, p) for j in range(pairs) for p in range(2) for h in range(2)])]
        + [Late()] * 4,
        [VM] * (3 + pairs),
        [shape_of((width, 2 * size), BF16)] * 2
        + [shape_of((pairs, size), F32)]
        + [shape_of((keys, size), BF16)] * pairs,
        (bits, g, g_far, inv, trig, weight, o_t, qkv, e, near, far, cosine, sine),
        [pltpu.VMEM((half, keys), BF16)],
        line=line,
        room=40,
        ahead=7,
        rank=rank,
    )


def input_terms_call(parts, weight, line=None):
    keys = parts[0].shape[0]
    rows = keys // 2
    _, width, half = weight.shape

    def body(*refs):
        ins, w, near, far = refs[:-3], refs[-3], refs[-2], refs[-1]
        for i, out in enumerate((near, far)):
            acc = 0.0
            for c in range(3):
                of = slice(c * PAIR, (c + 1) * PAIR)
                d = jnp.concatenate([part[i * rows : (i + 1) * rows, of] for part in ins], axis=1)
                acc = acc + dot(d, w[c], NT)
            out[...] = acc.astype(out.dtype)

    return call(
        body,
        (),
        [VM] * (len(parts) + 1),
        [VM] * 2,
        [shape_of((rows, width), F32), shape_of((rows, width), BF16)],
        (*parts, weight),
        line=line,
        room=12,
    )


def end_call(tokens, d_middle, near, far, vecs, line=None):
    rows, width = tokens.shape

    def body(tok, dm, dn, df, vec, grad_out, sum_out):
        normed, inverse = norm_parts(tok[...].astype(F32))
        d_in = dn[...] + df[...].astype(F32)
        grad_out[...] = (dm[...] + norm_back(d_in * vec[0:1], normed, inverse)).astype(BF16)
        sum_out[0:1] = total(d_in)
        sum_out[1:2] = total(d_in * normed)
        sum_out[2:8] = jnp.zeros((6, width), F32)

    return call(
        body,
        (),
        [VM] * 5,
        [VM] * 2,
        [pltpu.HBM((rows, width), BF16), shape_of((8, width), F32)],
        (tokens, d_middle, near, far, vecs),
        line=line,
    )


def swap(value):
    return lax.ppermute(value, "tensor", [(0, 1), (1, 0)])


def bit_swap(value, bit, order_by_core):
    pairs = []
    for place in range(lax.axis_size("dp")):
        for core in range(2):
            use = bit ^ core if order_by_core else bit
            pairs.append((place * 2 + core, (place ^ (1 << use)) * 2 + core))
    return lax.ppermute(value, ("dp", "tensor"), pairs)


def pick(value, index):
    return lax.dynamic_index_in_dim(value, index, 0, keepdims=False)


def join(mine, other, index):
    return jnp.where(index == 0, jnp.stack([mine, other]), jnp.stack([other, mine]))


def bit_count():
    return lax.axis_size("dp").bit_length() - 1


def pack_call(blocks, bit, line=None):
    width, size = blocks[0].shape

    def body(b, one, two, three, four, send, keep):
        def put(low, high):
            low[:, :size], low[:, size:] = one[...], two[...]
            high[:, :size], high[:, size:] = three[...], four[...]

        pl.when(b[0] == 0)(lambda: put(keep, send))
        pl.when(b[0] != 0)(lambda: put(send, keep))

    return call(
        body,
        (),
        [SM] + [VM] * 4,
        [VM, VM],
        [shape_of((width, 2 * size), BF16)] * 2,
        (bit, *blocks),
        line=line,
    )


def shared_call(end_sums, turn_sums, out_sums, down_sums, vecs, line=None):
    width = vecs.shape[1]

    def body(ends, turn, out, down, vec, rows):
        rows[0:1] = ends[0:1]
        rows[1:2] = ends[1:2] * vec[7:8]
        rows[2:4] = turn[0:2]
        rows[4:5] = turn[2:3] * vec[8:9]
        rows[5:6] = out[0:1]
        rows[6:7] = ends[1:2] * vec[9:10]
        rows[7:8] = turn[2:3] * vec[10:11]
        rows[8:9] = down[...]
        rows[9:16] = jnp.zeros((7, width), F32)

    return call(
        body,
        (),
        [VM] * 5,
        VM,
        shape_of((16, width), F32),
        (end_sums, turn_sums, out_sums, down_sums, vecs),
        line=line,
    )


def small_call(mine, other, b_up_sums, b_qkv_sums, line=None):
    width = mine.shape[1]
    half = width // 2

    def body(one, two, up_0, up_1, qkv_0, qkv_1, qkv_2, rows):
        rows[...] = jnp.concatenate(
            [
                (one[...] + two[...])[:9],
                up_0[...],
                up_1[...],
                jnp.concatenate([qkv_0[...], qkv_1[...]], axis=1),
                jnp.concatenate([qkv_2[...], jnp.zeros((1, half), F32)], axis=1),
                jnp.zeros((3, width), F32),
            ],
            axis=0,
        ).astype(BF16)

    return call(
        body,
        (),
        [VM] * 7,
        VM,
        shape_of((16, width), BF16),
        (mine, other, *b_up_sums, *b_qkv_sums),
        line=line,
    )


def append_call(mine, other, line=None):
    rows, width = mine.shape

    def body(one, two, out):
        out[:rows] = one[...]
        out[rows:] = two[...]

    return call(
        body, (), [VM, VM], VM, shape_of((2 * rows, width), BF16), (mine, other), line=line
    )


def split_add(mine, other, bit, line=None):
    rows, width = mine.shape

    def body(b, one, two, send, keep):
        field = (one[...].astype(F32) + two[...].astype(F32)).astype(BF16)
        low, high = field[: rows // 2], field[rows // 2 :]

        @pl.when(b[0] == 0)
        def _():
            keep[...] = low
            send[...] = high

        @pl.when(b[0] != 0)
        def _():
            send[...] = low
            keep[...] = high

    return call(
        body,
        (),
        [SM, VM, VM],
        [VM, VM],
        [shape_of((rows // 2, width), BF16)] * 2,
        (bit, mine, other),
        line=line,
    )


def plain_add(mine, other, line=None):
    def body(one, two, out):
        out[...] = (one[...].astype(F32) + two[...].astype(F32)).astype(BF16)

    return call(
        body, (), [VM, VM], VM, shape_of(mine.shape, BF16), (mine, other), line=line
    )


def stack_halves(mine, other, bit, line=None):
    rows, width = mine.shape

    def body(b, one, two, out):
        out[pl.ds(pl.multiple_of(b[0] * rows, rows), rows)] = one[...]
        out[pl.ds(pl.multiple_of((1 - b[0]) * rows, rows), rows)] = two[...]

    return call(
        body,
        (),
        [SM, VM, VM],
        VM,
        shape_of((2 * rows, width), BF16),
        (bit, mine, other),
        line=line,
    )


def unpack_call(mine, other, bit, before, units, at, line=None):
    width = mine.shape[0]
    size = mine.shape[1]

    def body(b, one, two, *rest):
        down_out, up_out = rest[-2:]

        @pl.when(b[0] == 0)
        def _():
            down_out[...] = one[...].astype(F32)
            up_out[...] = two[...].astype(F32)

        @pl.when(b[0] != 0)
        def _():
            down_out[...] = two[...].astype(F32)
            up_out[...] = one[...].astype(F32)

    extra = [pl.BlockSpec(memory_space=pl.ANY)] * len(before)
    return call(
        body,
        (1,),
        [SM, whole(mine.shape), whole(mine.shape)] + extra,
        [
            pl.BlockSpec((size, width), lambda i: (at, 0)),
            pl.BlockSpec((width, size), lambda i: (0, at)),
        ],
        [pltpu.HBM((units, width), F32), pltpu.HBM((width, units), F32)],
        (bit, mine, other) + tuple(far_core(x) for x in before),
        line=line,
        aliases={3: 0, 4: 1} if before else None,
        room=16,
    )


def unpack_last_call(mine, other, bit, line=None):
    width, size = mine.shape
    half = size // 2
    part = half // 3

    def body(b, one, two, qkv_out, out_out):
        def put(low, high):
            for c in range(3):

                @pl.when(pl.program_id(0) == c)
                def _():
                    for j, (block, at) in enumerate(((low, 0), (low, half), (high, 0))):
                        of = slice(at + c * PAIR, at + (c + 1) * PAIR)
                        qkv_out[0, :, j * PAIR : (j + 1) * PAIR] = block[:, of].astype(F32)
                    rows = slice(c * part, (c + 1) * part)
                    out_out[:, :half] = high[rows, half:].astype(F32)
                    out_out[:, half:] = high[slice(half + c * part, half + (c + 1) * part), half:].astype(F32)

        pl.when(b[0] == 0)(lambda: put(one, two))
        pl.when(b[0] != 0)(lambda: put(two, one))

    return call(
        body,
        (3,),
        [SM, whole(mine.shape), whole(mine.shape)],
        [pl.BlockSpec((1, width, half), lambda c: (c, 0, 0)), pl.BlockSpec((part, width), lambda c: (c, 0))],
        [pltpu.HBM((3, width, half), F32), pltpu.HBM((half, width), F32)],
        (bit, mine, other),
        line=line,
    )


def reduce_steps(send, keep, bits, halve, line):
    first, second, third = bits
    other = bit_swap(send, 0, True)
    yield other
    send, keep = split_add(keep, other, second, line)
    other = bit_swap(send, 1, True)
    yield other
    if halve:
        send, keep = split_add(keep, other, third, line)
        other = bit_swap(send, 2, False)
        yield other
        mine = plain_add(keep, other, line)
    else:
        mine = plain_add(keep, other, line)
        other = bit_swap(mine, 2, False)
        yield other
        mine = plain_add(mine, other, line)
    for bit in range(3, bit_count()):
        other = bit_swap(mine, bit, False)
        yield other
        mine = plain_add(mine, other, line)
    if halve:
        other = bit_swap(mine, 2, False)
        yield other
        mine = stack_halves(mine, other, third, line)
    other = bit_swap(mine, 1, True)
    yield other
    mine = stack_halves(mine, other, second, line)
    yield mine, bit_swap(mine, 0, True)


class Gather:
    def __init__(self, value, line):
        self.line = line
        self.value = value
        self.bit = 0
        self.other = bit_swap(value, 0, False)

    def go(self):
        if self.bit < bit_count():
            self.value = append_call(self.value, self.other, self.line)
            self.bit += 1
            if self.bit < bit_count():
                self.other = bit_swap(self.value, self.bit, False)

    def all(self):
        while self.bit < bit_count():
            self.go()
        return self.value


def tree_sum(value):
    while value.shape[0] > 1:
        value = value.reshape((-1, 2) + value.shape[1:])
        value = value[:, 0] + value[:, 1]
    return value[0]


class Line:
    def __init__(self):
        self.turn = jnp.zeros((8, 128), F32)

    def go(self):
        raise ValueError("unknown step")


class Group:
    def __init__(self, name, send, keep, bits, line, halve=True):
        self.name = name
        self.steps = reduce_steps(send, keep, bits, halve, line)
        with jax.named_scope(name):
            self.waiting = next(self.steps)

    def go(self):
        if not isinstance(self.waiting, tuple):
            self.waiting = next(self.steps)

    def halves(self):
        while not isinstance(self.waiting, tuple):
            self.go()
        return self.waiting


def shards(
    tokens,
    temb,
    lengths,
    w_mod,
    b_mod,
    gain_attn,
    query_key_value_weight,
    b_qkv,
    attention_output_weight,
    gain_mlp,
    up_weight,
    b_up,
    down_weight,
    b_down,
    cotangent,
):
    tokens, cotangent, length = tokens[0], cotangent[0], lengths[0]
    rows, width = tokens.shape
    core = lax.axis_index("tensor")
    place = lax.axis_index("dp")
    bits = [
        jnp.reshape((place >> b) & 1, (1,)).astype(jnp.int32) for b in (core, 1 - core, jnp.int32(2))
    ]
    half = width // 2
    start = core * rows
    counts = jnp.clip(jnp.stack([length - start, length - (rows - start)]), 0, rows)

    qkv_weight = jnp.swapaxes(query_key_value_weight, 0, 1)
    embed_part = lax.all_to_all(temb, "dp", split_axis=1, concat_axis=0, tiled=True)
    later, later_start, b_qkv, b_up, b_mod, b_down, gain_attn, gain_mlp, embed_part = lax.optimization_barrier(
        (tokens, start, b_qkv, b_up, b_mod, b_down, gain_attn, gain_mlp, embed_part)
    )
    qkv_bias = b_qkv.reshape(3, 1, half).astype(F32)
    up_bias = b_up.reshape(1, -1).astype(F32)
    normed_attn, _ = norm_parts(later.astype(F32))
    cosine, sine = rotary_tables(later_start, rows)
    mod_terms = jnp.dot(embed_part, w_mod, preferred_element_type=F32)
    mod_terms = lax.all_to_all(mod_terms, "dp", split_axis=0, concat_axis=0, tiled=True)
    mod_terms, cosine, sine, normed_attn, qkv_bias, up_bias = lax.optimization_barrier(
        (mod_terms, cosine, sine, normed_attn, qkv_bias, up_bias)
    )
    modulation = jnp.sum(mod_terms, axis=0) + b_mod.astype(F32)
    shift_attn, scale_attn, gate_attn, shift_mlp, scale_mlp, gate_mlp = modulation.reshape(6, width)
    gain_attn = gain_attn.astype(F32)
    gain_mlp = gain_mlp.astype(F32)
    vecs = jnp.stack(
        [
            gain_attn * (1.0 + scale_attn),
            shift_attn,
            gate_attn,
            gain_mlp * (1.0 + scale_mlp),
            shift_mlp,
            gate_mlp,
            b_down.astype(F32),
            gain_attn,
            gain_mlp,
            1.0 + scale_attn,
            1.0 + scale_mlp,
        ]
    )

    attn_in, x_near = input_call(normed_attn, vecs)
    attn_in_far = swap(attn_in)
    g_mlp, down_sums = upstream_call(counts, cotangent, vecs)
    g_mlp_far = swap(g_mlp)
    e, o_t, inv, branch_near, branch_far, qkv, trig = attend_call(
        counts, attn_in, attn_in_far, qkv_weight, qkv_bias, cosine, sine, attention_output_weight
    )
    attn_branch, fed = middle_call(tokens, branch_near, swap(branch_far), vecs)
    fed_far = swap(fed)
    up_weight, down_weight = carry_call(fed, up_weight, down_weight)
    units = up_weight.shape[1]
    size = units // 2
    line = Line()
    b_up_sums, groups, made = [], {}, {}
    before = ()
    for part, name in enumerate(("mlp_first", "mlp_second")):
        send, keep, b_up_sum, *before = mlp_call(
            part * size, size, bits[0], fed, fed_far, g_mlp, g_mlp_far, up_weight, down_weight, up_bias, before, line
        )
        groups[name] = Group(name, send, keep, bits, line)
        b_up_sums.append(b_up_sum)
    made["d_near"], d_far, made["b_near"], b_far = before
    made["d_far"] = swap(d_far)
    made["b_far"] = swap(b_far)

    def turn():
        made["d_middle"], g_attn, made["turn_sums"] = turn_call(
            counts, tokens, cotangent, attn_branch, made["d_near"], made["d_far"], vecs, line
        )
        made["g"] = (g_attn, swap(g_attn))
        made["x_far"] = swap(lax.optimization_barrier((x_near, g_attn))[0])

    def back():
        send, keep, sums, *made["d_alls"] = attend_back_call(
            bits[0], *made["g"], attention_output_weight, qkv, e, o_t, inv, trig, cosine, sine, x_near, made["x_far"], line
        )
        made["b_qkv"] = [sums[n : n + 1] for n in range(sums.shape[0])]
        groups["projections"] = Group("projections", send, keep, bits, line)

    def d_attn_in():
        made["a_near"], a_far = input_terms_call(made["d_alls"], qkv_weight, line)
        made["a_far"] = swap(a_far)

    def finish():
        made["output"], made["out_sums"] = finish_call(
            counts, tokens, cotangent, attn_branch, made["b_near"], made["b_far"], vecs, line
        )

    def end():
        made["grad_tokens"], made["end_sums"] = end_call(
            tokens, made["d_middle"], made["a_near"], made["a_far"], vecs, line
        )

    def share():
        shared = shared_call(made["end_sums"], made["turn_sums"], made["out_sums"], down_sums, vecs, line)
        made["shared"] = (shared, swap(shared))

    def small():
        rows = small_call(*made["shared"], b_up_sums, made["b_qkv"], line)
        groups["small"] = Gather(rows, line)

    def unpack(at, name):
        made["totals"] = unpack_call(*groups[name].halves(), bits[0], made.get("totals", ()), units, at, line)

    def mod_back():
        every, line.turn = lax.optimization_barrier((groups["small"].all().reshape(-1, 16, width), line.turn))
        grad_mod_all = every[:, :6].reshape(-1, 6 * width)
        embed_order = lax.iota(jnp.int32, every.shape[0]) ^ place
        embed_here = jnp.take(embed_part, embed_order, axis=0)
        made["grad_w_mod"] = dot(embed_here, grad_mod_all, TN)
        embed_terms = jnp.take(dot(grad_mod_all, w_mod, NT), embed_order, axis=0)
        made["grad_temb"] = lax.all_to_all(embed_terms, "dp", split_axis=0, concat_axis=1, tiled=True)
        made["sums"] = tree_sum(every.astype(F32))

    acts = [turn, back, d_attn_in, finish, end, share, small, mod_back]
    acts = {act.__name__: act for act in acts}
    gather = acts.pop("small")
    acts["begin"] = gather
    acts["unpack_first"] = lambda: unpack(0, "mlp_first")
    acts["unpack_second"] = lambda: unpack(1, "mlp_second")
    for word in ORDER:
        with jax.named_scope(word):
            acts.get(word, groups.get(word, line).go)()
    groups["projections"].halves()
    grad_temb, grad_w_mod, sums = made["grad_temb"], made["grad_w_mod"], made["sums"]
    output, grad_tokens, totals = made["output"], made["grad_tokens"], made["totals"]
    down_total, up_total = totals
    qkv_total, out_total = unpack_last_call(*groups["projections"].halves(), bits[0], line)
    b_up_total = sums[9:11].reshape(-1)
    b_qkv_total = sums[11:13].reshape(-1)[: 9 * PAIR].reshape(3, 3, PAIR)
    return (
        output[None],
        grad_tokens[None],
        grad_temb,
        grad_w_mod,
        sums[:6].reshape(-1),
        sums[6],
        jnp.swapaxes(qkv_total, 0, 1),
        jnp.swapaxes(b_qkv_total, 0, 1).reshape(3, half),
        out_total,
        sums[7],
        up_total,
        b_up_total,
        down_total,
        sums[8],
    )


def solution(mesh):
    return jax.shard_map(
        shards,
        mesh=mesh,
        in_specs=(
            P("dp", "tensor", None),
            P("dp", None),
            P("dp"),
            P("dp", None),
            P(),
            P(),
            P(None, None, "tensor"),
            P(None, "tensor"),
            P("tensor", None),
            P(),
            P(None, "tensor"),
            P("tensor"),
            P("tensor", None),
            P(),
            P("dp", "tensor", None),
        ),
        out_specs=(
            P("dp", "tensor", None),
            P("dp", "tensor", None),
            P("dp", None),
            P("dp", None),
            P(),
            P(),
            P(None, None, "tensor"),
            P(None, "tensor"),
            P("tensor", None),
            P(),
            P(None, "tensor"),
            P("tensor"),
            P("tensor", None),
            P(),
        ),
        check_vma=False,
    )
```
